128 devices in a mesh: row: 8 (over z, core), col: 16 (over y, x).
Axes of the slice: x: 4, y: 4, z: 4, core: 2. Of those that a mesh axis runs over, the one named last changes fastest.
Arguments:
- fem_basis: float32 [2, 16, 2, 262144], P(None, None, None, ('row', 'col')), may hold values from -8 to 8
- bem_basis: float32 [2, 16, 2, 16384], P(None, None, None, ('row', 'col')), may hold values from -8 to 8
- fem_diagonal: float32 [262144], P(('row', 'col')), may hold values from 1 to 4
- fem_values: float32 [16, 262144], P(None, ('row', 'col')), may hold values from -1.5 to 1.5
- fem_columns: int32 [16, 262144], P(None, ('row', 'col')), may hold values from 0 to 2559
- halo_rows: int32 [4, 16384], P(None, ('row', 'col')), may hold values from 0 to 2047
- bem_matrix: bfloat16 [2, 16384, 16384], P(None, 'row', 'col'), may hold values from -0.03125 to 0.03125
- trace_rows: int32 [32768], P(('row', 'col')), may hold values from -1 to 2047, as said below
- bem_slot: int32 [16384], P(('row', 'col')), may hold values from 0 to 255, as said below
Outputs:
- next_fem: float32 [16, 2, 262144], P(None, None, ('row', 'col'))
- next_bem: float32 [16, 2, 16384], P(None, None, ('row', 'col'))
- hessenberg: float32 [2, 16, 16], replicated
- r_factor: float32 [16, 16], replicated
The draws below stay inside these ranges and needn't reach their ends.
Inputs may be any that keep to these rules, and one draw needn't show every extreme that they name: `trace_rows`: each device's entries form one block of 2 slots per BEM owner, owners in row+col order; a block is all -1 (unused) or holds local FEM rows, the rows of one device being distinct; every owner is fed by exactly 64 full blocks. `bem_slot`: value = source device along row+col times 2 plus slot; within one owner the values are distinct and are exactly the full slots that trace_rows sends to that owner.
All inputs are finite; a program needn't handle non-finite values.
Results may differ from the reference program's by a relative error of at most 0.0014.
Values may be sent and summed in bfloat16 or wider, within the bound.
A program may use at most 128 MiB of HBM per device.

```python
import math
import jax
import jax.numpy as jnp
from jax import lax

NRHS = 16
BLOCKS = 2
NZ = 16
ROWS_DEV = 2048
NBEM = 16384
HALO = 128
PIECE = 128
PICK = 64
TSLOT = 2
SLOTS = 256
NFEM = 262144
N_ROW = 8
N_COL = 16
DEVICES = 128


def basis_draw(key, length):
    extent = (BLOCKS, NRHS, 2, length)
    common = jax.random.normal(jax.random.fold_in(key, 11), (1, NRHS, 2, length), jnp.float32)
    private = jax.random.normal(jax.random.fold_in(key, 12), extent, jnp.float32)
    return jnp.clip((private + 0.7 * common) / 1.22, -8.0, 8.0)


def draw_fem_basis(key, part):
    return basis_draw(key, NFEM)


def draw_bem_basis(key, part):
    return basis_draw(jax.random.fold_in(key, 5), NBEM)


def trace_plan(key):
    base = jax.random.fold_in(key, 29)
    levels = jax.random.randint(jax.random.fold_in(base, 1), (DEVICES,), 0, 4) * 96
    jitter = jax.random.randint(jax.random.fold_in(base, 2), (DEVICES, DEVICES), 0, 256)
    sources = jnp.arange(DEVICES, dtype=jnp.int32)
    scores = (levels[None, :] + jitter) * DEVICES + sources[None, :]
    picked = lax.top_k(scores, PICK)[1].astype(jnp.int32)
    order_keys = jax.random.randint(jax.random.fold_in(base, 3), (DEVICES, PIECE), 0, 1 << 20) * PIECE + jnp.arange(PIECE, dtype=jnp.int32)[None, :]
    placing = jnp.argsort(order_keys, axis=1).astype(jnp.int32)
    inverse = jnp.argsort(placing, axis=1).astype(jnp.int32)
    slot_of_position = (picked[:, :, None] * TSLOT + jnp.arange(TSLOT, dtype=jnp.int32)[None, None, :]).reshape(DEVICES, PIECE)
    slot_table = jnp.take_along_axis(slot_of_position, inverse, axis=1)
    row_keys = jax.random.randint(jax.random.fold_in(base, 4), (DEVICES, ROWS_DEV), 0, 1 << 12) * ROWS_DEV + jnp.arange(ROWS_DEV, dtype=jnp.int32)[None, :]
    rows_order = jnp.argsort(row_keys, axis=1)[:, :SLOTS].astype(jnp.int32)
    chosen = jnp.any(picked[:, :, None] == sources[None, None, :], axis=1)
    chosen_rows = jnp.repeat(chosen.T, TSLOT, axis=1)
    rows_table = jnp.where(chosen_rows, rows_order, -1).astype(jnp.int32)
    return (rows_table.reshape(-1), slot_table.reshape(-1))


def draw_trace_rows(key, part):
    return trace_plan(key)[0]


def draw_bem_slot(key, part):
    return trace_plan(key)[1]


def with_ends(array, key, smallest, high):
    place = [jax.random.randint(jax.random.fold_in(key, axis), (), 0, length) for axis, length in enumerate(array.shape)]
    main_axis = array.shape.index(max(array.shape))
    beside = place[:main_axis] + [(place[main_axis] + 1) % array.shape[main_axis]] + place[main_axis + 1:]
    return array.at[tuple(place)].set(smallest).at[tuple(beside)].set(high)


def level_of(rng, shape, split, least, high):
    gain = 1.0
    for dim, shards_of in split:
        steps = jax.random.uniform(jax.random.fold_in(jax.random.fold_in(rng, 6), dim), (shards_of,), jnp.float32, least / len(split), high / len(split))
        gain = gain * jnp.repeat(jnp.exp(steps), shape[dim] // shards_of).reshape((-1,) + (1,) * (len(shape) - 1 - dim))
    return gain


def bell_draw(own_key, shape, spread, bound, cuts=(), kind=jnp.bfloat16):
    level = level_of(own_key, shape, cuts, -0.22, 0.18) if cuts else 1.0
    drawn = jax.random.normal(own_key, shape, jnp.float32) * spread * level
    return jnp.minimum(jnp.maximum(drawn, -bound), bound).astype(kind)


def setup_inputs(seed: int = 0) -> dict:
    arg_keys = jax.random.split(jax.random.key(seed), 10)
    return {
        "fem_basis": draw_fem_basis(jax.random.fold_in(arg_keys[9], 71), 0),
        "bem_basis": draw_bem_basis(jax.random.fold_in(arg_keys[9], 71), 0),
        "fem_diagonal": jnp.clip(jnp.exp(math.log(4.0) - 1.3862944 * jax.random.uniform(arg_keys[2], (NFEM,), jnp.float32) ** level_of(arg_keys[2], (NFEM,), ((0, 128),), -0.2, 0.2)), 1.0, 4.0),
        "fem_values": bell_draw(arg_keys[3], (NZ, NFEM), NZ ** -0.5, 1.5, ((1, 128),), jnp.float32),
        "fem_columns": with_ends(jax.random.randint(arg_keys[4], (NZ, NFEM), 0, ROWS_DEV + 4 * HALO), jax.random.fold_in(arg_keys[4], 1), 0, (ROWS_DEV + 4 * HALO) - 1).astype(jnp.int32),
        "halo_rows": with_ends(jax.random.randint(arg_keys[5], (4, DEVICES * HALO), 0, ROWS_DEV), jax.random.fold_in(arg_keys[5], 1), 0, ROWS_DEV - 1).astype(jnp.int32),
        "bem_matrix": bell_draw(arg_keys[6], (2, NBEM, NBEM), (2 * NBEM) ** -0.5, 0.03125, ((1, 8), (2, 16))),
        "trace_rows": draw_trace_rows(jax.random.fold_in(arg_keys[9], 71), 0),
        "bem_slot": draw_bem_slot(jax.random.fold_in(arg_keys[9], 71), 0),
    }


HIGHEST = lax.Precision.HIGHEST

def dotted(lefts, rights):
    return lax.dot_general(lefts.reshape(lefts.shape[0], -1).astype(jnp.float32), rights.reshape(rights.shape[0], -1).astype(jnp.float32), (((1,), (1,)), ((), ())), precision=HIGHEST, preferred_element_type=jnp.float32)

def combine(coeffs, basis):
    flat_basis = basis.reshape(basis.shape[0], -1)
    merged = lax.dot_general(coeffs.astype(jnp.float32), flat_basis.astype(jnp.float32), (((0,), (0,)), ((), ())), precision=HIGHEST, preferred_element_type=jnp.float32)
    return merged.reshape((coeffs.shape[1],) + basis.shape[1:])

def shifted(blocks, axis_pos, forward):
    widths = [(0, 0)] * blocks.ndim
    widths[axis_pos] = (1, 0) if forward else (0, 1)
    padded = jnp.pad(blocks, widths)
    if forward:
        return lax.slice_in_dim(padded, 0, blocks.shape[axis_pos], axis=axis_pos)
    return lax.slice_in_dim(padded, 1, blocks.shape[axis_pos] + 1, axis=axis_pos)

def fem_apply(vectors, fem_diagonal, fem_values, fem_columns, halo_rows):
    lists = halo_rows.reshape(4, N_ROW, N_COL, HALO)
    values = fem_values.reshape(NZ, N_ROW, N_COL, ROWS_DEV)
    columns = fem_columns.reshape(NZ, N_ROW, N_COL, ROWS_DEV)
    diagonal = fem_diagonal.reshape(N_ROW, N_COL, ROWS_DEV)

    def single(one_vector):
        outbound = [jnp.take_along_axis(one_vector, lists[direction], axis=2) for direction in range(4)]
        extended = jnp.concatenate([one_vector, shifted(outbound[0], 1, True), shifted(outbound[1], 1, False), shifted(outbound[2], 0, True), shifted(outbound[3], 0, False)], axis=2)

        def accumulate(position, accrued):
            return accrued + values[position] * jnp.take_along_axis(extended, columns[position], axis=2)
        return lax.fori_loop(0, NZ, accumulate, diagonal * one_vector)
    stacked = vectors.reshape(NRHS * 2, N_ROW, N_COL, ROWS_DEV)
    return lax.map(single, stacked).reshape(NRHS, 2, NFEM)

def bem_apply(vectors, bem_matrix):
    piece_len = NBEM // (N_ROW * N_COL)
    rounded = vectors.astype(jnp.bfloat16).reshape(NRHS * 2, N_ROW, N_COL, piece_len)
    stored = jnp.transpose(rounded, (0, 2, 1, 3)).reshape(NRHS * 2, NBEM)
    real_mat = lax.dot_general(stored.astype(jnp.float32), bem_matrix[0].astype(jnp.float32), (((1,), (1,)), ((), ())), preferred_element_type=jnp.float32).reshape(NRHS, 2, NBEM)
    imag_mat = lax.dot_general(stored.astype(jnp.float32), bem_matrix[1].astype(jnp.float32), (((1,), (1,)), ((), ())), preferred_element_type=jnp.float32).reshape(NRHS, 2, NBEM)
    return jnp.stack([real_mat[:, 0] - imag_mat[:, 1], imag_mat[:, 0] + real_mat[:, 1]], axis=1)

def trace_index(trace_rows, bem_slot):
    piece_len = NBEM // (N_ROW * N_COL)
    owners = jnp.arange(NBEM, dtype=jnp.int32) // piece_len
    sources = bem_slot // TSLOT
    within = bem_slot % TSLOT
    rows_at = trace_rows[sources * SLOTS + owners * TSLOT + within]
    return (sources * ROWS_DEV + rows_at).astype(jnp.int32)

def reference(fem_basis, bem_basis, fem_diagonal, fem_values, fem_columns, halo_rows, bem_matrix, trace_rows, bem_slot):
    fem_last = fem_basis[BLOCKS - 1]
    bem_last = bem_basis[BLOCKS - 1]
    positions = trace_index(trace_rows, bem_slot)
    fem_image = fem_apply(fem_last, fem_diagonal, fem_values, fem_columns, halo_rows)
    bem_image = bem_apply(bem_last, bem_matrix) + fem_last[:, :, positions]
    fem_image = fem_image.at[:, :, positions].add(bem_last)
    count = 2.0 * (NFEM + NBEM)
    fem_flat = fem_basis.reshape(BLOCKS * NRHS, 2, NFEM)
    bem_flat = bem_basis.reshape(BLOCKS * NRHS, 2, NBEM)
    coeffs_one = (dotted(fem_flat, fem_image) + dotted(bem_flat, bem_image)) / count
    fem_once = fem_image - combine(coeffs_one, fem_flat)
    bem_once = bem_image - combine(coeffs_one, bem_flat)
    coeffs_two = (dotted(fem_flat, fem_once) + dotted(bem_flat, bem_once)) / count
    fem_twice = fem_once - combine(coeffs_two, fem_flat)
    bem_twice = bem_once - combine(coeffs_two, bem_flat)
    gram_matrix = (dotted(fem_twice, fem_twice) + dotted(bem_twice, bem_twice)) / count
    lower_factor = jnp.linalg.cholesky(gram_matrix)
    inverse_lower = jax.scipy.linalg.solve_triangular(lower_factor, jnp.eye(NRHS, dtype=jnp.float32), lower=True)
    next_fem = combine(inverse_lower.T, fem_twice)
    next_bem = combine(inverse_lower.T, bem_twice)
    hessenberg = (coeffs_one + coeffs_two).reshape(BLOCKS, NRHS, NRHS)
    return (next_fem, next_bem, hessenberg, lower_factor.T)
```

```python
import functools

import jax
import jax.numpy as jnp
from jax import lax
from jax.experimental import pallas as pl
from jax.experimental.pallas import tpu as pltpu
from jax.sharding import PartitionSpec as P

F32 = jnp.float32
BF16 = jnp.bfloat16
MESH = pl.DeviceIdType.MESH
HIGHEST = lax.Precision.HIGHEST
ROWS, COLS = 8, 16
DEVICES = ROWS * COLS
VEC = 32
LOCAL = 2048
PIECE = 128
WIDE = LOCAL + PIECE
COUNT = 2.0 * DEVICES * (LOCAL + PIECE)
NT = (((1,), (1,)), ((), ()))


def split2(x):
    high = x.astype(BF16)
    return high, (x - high.astype(F32)).astype(BF16)


def split3(x):
    high = x.astype(BF16)
    rest = x - high.astype(F32)
    mid = rest.astype(BF16)
    return high, mid, (rest - mid.astype(F32)).astype(BF16)


def lane_gather(table, lanes):
    return jnp.take_along_axis(table, lanes, axis=1, mode="promise_in_bounds")


def small_dot(a, b, dims):
    return lax.dot_general(a, b, (dims, ((), ())), precision=HIGHEST, preferred_element_type=F32)


def kernel(
    fem, bem, diag, vals, cols, halo, mat, trace, slot,
    next_fem, next_bem, hess, rfac,
    pieces, halo_out, halo_in, phi, partial, arrived, swap_out, swap_in,
    mat_buf, image, zp, pack, sum_out, col_in, row_in,
    mat_sem, halo_send, halo_recv, phi_send, phi_recv, part_send, part_recv,
    swap_send, swap_recv, col_send, col_recv, row_send, row_recv,
):
    r = lax.axis_index("row")
    c = lax.axis_index("col")
    me = r * COLS + c

    def matrix_copy(k):
        chunk = lax.rem(k + c // 2, 8)
        rows = pl.ds(pl.multiple_of(chunk * 256, 256), 256)
        return pltpu.make_async_copy(mat.at[:, rows, :], mat_buf.at[:, rows, :], mat_sem.at[k])

    for k in range(8):
        matrix_copy(k).start()

    def remote(src, dst, send, recv, row, col):
        return pltpu.make_async_remote_copy(
            src_ref=src, dst_ref=dst, send_sem=send, recv_sem=recv,
            device_id={"row": row, "col": col}, device_id_type=MESH,
        )

    def wait_bytes(ref, sem):
        pltpu.make_async_copy(ref, ref, sem).wait()

    phi_mine = bem[1].astype(BF16)
    mine = pl.ds(pl.multiple_of(r * PIECE, PIECE), PIECE)
    phi[:, mine] = phi_mine

    def send_phi(k, _):
        other = lax.rem(r + k, ROWS)
        remote(phi.at[:, mine], phi.at[:, mine], phi_send, phi_recv, other, c).start()
        return 0

    lax.fori_loop(1, ROWS, send_phi, 0)

    def picked(rows):
        rows = jnp.broadcast_to(rows, (VEC, 128))
        high = rows >> 7
        low = rows & 127
        out = jnp.zeros((VEC, 128), F32)
        for t in range(LOCAL // 128):
            out = jnp.where(high == t, lane_gather(fem[1, :, t * 128 : (t + 1) * 128], low), out)
        return out

    lane = lax.broadcasted_iota(jnp.int32, (8, 128), 1)
    trace_lo = jnp.broadcast_to(trace[:, :128], (8, 128))
    trace_hi = jnp.broadcast_to(trace[:, 128:], (8, 128))
    trace_q = []
    for q in range(2):
        source = (2 * lane + q) & 127
        full = jnp.where(lane < 64, lane_gather(trace_lo, source), lane_gather(trace_hi, source))
        trace_q.append(full[:1])

    for d in range(4):
        halo_out[d] = picked(halo[d : d + 1, :])

    for d, missing in enumerate((c == 0, c == COLS - 1, r == 0, r == ROWS - 1)):

        @pl.when(missing)
        def _(d=d):
            halo_in[d] = jnp.zeros((VEC, 128), F32)

    @pl.when(c + 1 < COLS)
    def _():
        remote(halo_out.at[0], halo_in.at[0], halo_send.at[0], halo_recv.at[0], r, c + 1).start()

    @pl.when(c > 0)
    def _():
        remote(halo_out.at[1], halo_in.at[1], halo_send.at[1], halo_recv.at[1], r, c - 1).start()

    @pl.when(r + 1 < ROWS)
    def _():
        remote(halo_out.at[2], halo_in.at[2], halo_send.at[2], halo_recv.at[2], r + 1, c).start()

    @pl.when(r > 0)
    def _():
        remote(halo_out.at[3], halo_in.at[3], halo_send.at[3], halo_recv.at[3], r - 1, c).start()

    leaving = [picked(jnp.maximum(t, 0)) * (t >= 0).astype(F32) for t in trace_q]
    owner = lax.broadcasted_iota(jnp.int32, (2 * DEVICES, PIECE), 0)
    owner = jnp.where(owner < DEVICES, 2 * owner, 2 * (owner - DEVICES) + 1)
    places = (owner == slot[...]).astype(F32).astype(BF16)
    back = lax.dot_general(
        jnp.concatenate(split3(bem[1]), axis=0), places, NT, preferred_element_type=F32
    )
    back = back[:VEC] + back[VEC : 2 * VEC] + back[2 * VEC :]
    swap_out[...] = jnp.concatenate(leaving + [back[:, :128], back[:, 128:]], axis=0).T

    def send_swap(k, _):
        other = lax.rem(me + k, DEVICES)
        remote(
            swap_out.at[pl.ds(other, 1)], swap_in.at[pl.ds(me, 1)], swap_send, swap_recv,
            other // COLS, lax.rem(other, COLS),
        ).start()
        return 0

    lax.fori_loop(1, DEVICES, send_swap, 0)
    swap_in[pl.ds(me, 1)] = swap_out[pl.ds(me, 1)]

    for p in range(2):
        for b in range(2):
            rows = slice(b * 16, b * 16 + 16)
            part = slice(p * 16, p * 16 + 16)
            for a, x in enumerate(split3(fem[b, part, :])):
                zp[p, a * 48 + b * 16 : a * 48 + b * 16 + 16, :LOCAL] = x
            for a, x in enumerate(split3(bem[b, part, :])):
                zp[p, a * 48 + b * 16 : a * 48 + b * 16 + 16, LOCAL:] = x
    own = jnp.zeros((VEC, VEC), F32)
    for p in range(2):
        whole = jnp.concatenate([zp[p, a * 48 : a * 48 + 32, :] for a in range(3)], axis=0)
        for b in range(3):
            both = lax.dot_general(
                whole, zp[p, b * 48 : b * 48 + 32, :], NT, preferred_element_type=F32
            )
            own = own + both[:32] + both[32:64] + both[64:]
    pack[...] = jnp.zeros((48, 128), F32)
    pack[:32, :32] = own
    packed = pack[0:8, :]
    for g in range(1, 4):
        packed = packed + pltpu.roll(pack[8 * g : 8 * g + 8, :], 32 * g, 1)
    sum_out[0] = packed

    def reduce_cols(n):
        col_in[n, c] = sum_out[n]

        def send(k, _):
            other = lax.rem(c + k, COLS)
            remote(sum_out.at[n], col_in.at[n, c], col_send.at[n], col_recv.at[n], r, other).start()
            return 0

        lax.fori_loop(1, COLS, send, 0)

    def reduce_rows(n):
        wait_bytes(col_in.at[n, pl.ds(0, COLS - 1)], col_recv.at[n])
        total = col_in[n, 0]
        for k in range(1, COLS):
            total = total + col_in[n, k]
        row_in[n, r] = total

        def send(k, _):
            other = lax.rem(r + k, ROWS)
            remote(row_in.at[n, r], row_in.at[n, r], row_send.at[n], row_recv.at[n], other, c).start()
            return 0

        lax.fori_loop(1, ROWS, send, 0)

    def reduced(n):
        wait_bytes(row_in.at[n, pl.ds(0, ROWS - 1)], row_recv.at[n])
        total = row_in[n, 0]
        for k in range(1, ROWS):
            total = total + row_in[n, k]
        return total * (1.0 / COUNT)

    reduce_cols(0)

    wait_bytes(phi.at[:, pl.ds(0, (ROWS - 1) * PIECE)], phi_recv)
    phi_all = phi[...]
    turned = jnp.concatenate([-phi_all[16:], phi_all[:16]], axis=0)

    def multiply(k, _):
        chunk = lax.rem(k + c // 2, 8)
        matrix_copy(k).wait()
        rows = pl.ds(pl.multiple_of(chunk * 256, 256), 256)
        out = lax.dot_general(phi_all, mat_buf[0, rows, :], NT, preferred_element_type=F32)
        out = out + lax.dot_general(turned, mat_buf[1, rows, :], NT, preferred_element_type=F32)
        for half in range(2):
            other = 2 * chunk + half
            partial[other] = out[:, half * 128 : half * 128 + 128]

            @pl.when(other != c)
            def _():
                remote(partial.at[other], arrived.at[c], part_send, part_recv, r, other).start()

        return 0

    lax.fori_loop(0, 8, multiply, 0)
    arrived[c] = partial[c]
    reduce_rows(0)

    @pl.when(c > 0)
    def _():
        wait_bytes(halo_in.at[0], halo_recv.at[0])

    @pl.when(c + 1 < COLS)
    def _():
        wait_bytes(halo_in.at[1], halo_recv.at[1])

    @pl.when(r > 0)
    def _():
        wait_bytes(halo_in.at[2], halo_recv.at[2])

    @pl.when(r + 1 < ROWS)
    def _():
        wait_bytes(halo_in.at[3], halo_recv.at[3])

    for t in range(10):
        if t < 8:
            x = fem[1, :, t * 256 : (t + 1) * 256]
        else:
            x = jnp.concatenate([halo_in[2 * t - 16], halo_in[2 * t - 15]], axis=1)
        for a, piece in enumerate(split2(x)):
            pieces[a, t * 32 : t * 32 + 32, :] = piece

    def product(j, _):
        here = pl.ds(pl.multiple_of(j * 256, 256), 256)
        acc = diag[:, here] * fem[1, :, here]
        for k in range(16):
            column = cols[k : k + 1, here]
            low = column & 255
            high = column >> 8
            hot = (lax.broadcasted_iota(jnp.int32, (256, 256), 0) == low).astype(F32).astype(BF16)
            found = jnp.dot(pieces[0], hot, preferred_element_type=F32)
            found = found + jnp.dot(pieces[1], hot, preferred_element_type=F32)
            got = found[:32]
            for t in range(1, 10):
                got = jnp.where(
                    jnp.broadcast_to(high == t, (32, 256)), found[t * 32 : t * 32 + 32], got
                )
            acc = acc + vals[k : k + 1, here] * got
        image[:, here] = acc
        return 0

    lax.fori_loop(0, LOCAL // 256, product, 0)

    wait_bytes(swap_in.at[pl.ds(0, DEVICES - 1)], swap_recv)
    met = swap_in[...].T
    chosen = jnp.broadcast_to(slot[...], (VEC, PIECE))
    taken = jnp.where(
        (chosen & 1) == 0, lane_gather(met[:32], chosen >> 1), lane_gather(met[32:64], chosen >> 1)
    )
    answers = jnp.concatenate([met[64:96], met[96:]], axis=1)
    answers = jnp.concatenate(split3(answers), axis=0)
    targets = jnp.concatenate(trace_q, axis=1)
    for t in range(LOCAL // 256):
        row = lax.broadcasted_iota(jnp.int32, (256, 256), 0) + t * 256
        hot = (row == targets).astype(F32).astype(BF16)
        put = lax.dot_general(answers, hot, NT, preferred_element_type=F32)
        here = slice(t * 256, t * 256 + 256)
        image[:, here] = image[:, here] + put[:32] + put[32:64] + put[64:]
    wait_bytes(arrived.at[pl.ds(0, COLS - 1)], part_recv)
    bem_image = taken
    for k in range(COLS):
        bem_image = bem_image + arrived[k]
    for p in range(2):
        part = slice(p * 16, p * 16 + 16)
        for a, x in enumerate(split3(image[part, :])):
            zp[p, a * 48 + 32 : a * 48 + 48, :LOCAL] = x
        for a, x in enumerate(split3(bem_image[part, :])):
            zp[p, a * 48 + 32 : a * 48 + 48, LOCAL:] = x

    inner = jnp.zeros((48, 16), F32)
    for p in range(2):
        whole = zp[p]
        for b in range(3):
            both = lax.dot_general(
                whole, zp[p, b * 48 + 32 : b * 48 + 48, :], NT, preferred_element_type=F32
            )
            inner = inner + both[:48] + both[48:96] + both[96:]
    pack[...] = jnp.zeros((48, 128), F32)
    pack[:, :16] = inner
    packed = pack[0:8, :]
    for g in range(1, 6):
        packed = packed + pltpu.roll(pack[8 * g : 8 * g + 8, :], 16 * g, 1)
    sum_out[1] = packed
    reduce_cols(1)
    total = reduced(0)
    for g in range(4):
        pack[8 * g : 8 * g + 8, :] = total if g == 0 else pltpu.roll(total, 128 - 32 * g, 1)
    gram_q = pack[:32, :32]
    reduce_rows(1)
    total = reduced(1)
    for g in range(6):
        pack[8 * g : 8 * g + 8, :] = total if g == 0 else pltpu.roll(total, 128 - 16 * g, 1)
    one = pack[:32, :16]
    norm = pack[32:48, :16]

    both = 2.0 * one - small_dot(gram_q, one, ((1,), (0,)))
    hess[...] = both
    left = small_dot(gram_q, both, ((1,), (0,))) - one
    gram = norm + small_dot(both, left, ((0,), (0,))) - small_dot(one, both, ((0,), (0,)))
    row_id = lax.broadcasted_iota(jnp.int32, (16, 16), 0)
    col_id = lax.broadcasted_iota(jnp.int32, (16, 16), 1)
    work = (gram + gram.T) * 0.5
    inverse = (row_id == col_id).astype(F32)
    upper = jnp.zeros((16, 16), F32)
    lower_inv = jnp.zeros((16, 16), F32)
    for j in range(16):
        pivot = work[j : j + 1, j : j + 1]
        root = lax.rsqrt(pivot)
        root = root * (1.5 - 0.5 * pivot * root * root)
        line = jnp.broadcast_to(work[j : j + 1, :] * root, (16, 16))
        line_inv = jnp.broadcast_to(inverse[j : j + 1, :] * root, (16, 16))
        column = jnp.broadcast_to(work[:, j : j + 1] * root, (16, 16))
        upper = jnp.where((row_id == j) & (col_id >= j), line, upper)
        lower_inv = jnp.where(row_id == j, line_inv, lower_inv)
        work = work - column * line
        inverse = inverse - column * line_inv
    rfac[...] = upper

    weights = -small_dot(lower_inv, both, ((1,), (1,)))
    w_high, w_low = split2(weights)
    l_high, l_low = split2(lower_inv)
    w_pair = jnp.concatenate([w_high, w_low], axis=0)
    l_pair = jnp.concatenate([l_high, l_low], axis=0)
    for p in range(2):
        first = jnp.dot(w_pair, zp[p, 0:32, :], preferred_element_type=F32)
        first = first + jnp.dot(l_pair, zp[p, 32:48, :], preferred_element_type=F32)
        second = jnp.dot(w_high, zp[p, 48:80, :], preferred_element_type=F32)
        second = second + jnp.dot(l_high, zp[p, 80:96, :], preferred_element_type=F32)
        made = first[:16] + first[16:] + second
        next_fem[p] = made[:, :LOCAL]
        next_bem[p] = made[:, LOCAL:]

    @pl.when(c + 1 < COLS)
    def _():
        wait_bytes(halo_out.at[0], halo_send.at[0])

    @pl.when(c > 0)
    def _():
        wait_bytes(halo_out.at[1], halo_send.at[1])

    @pl.when(r + 1 < ROWS)
    def _():
        wait_bytes(halo_out.at[2], halo_send.at[2])

    @pl.when(r > 0)
    def _():
        wait_bytes(halo_out.at[3], halo_send.at[3])

    wait_bytes(phi.at[:, pl.ds(0, (ROWS - 1) * PIECE)], phi_send)
    wait_bytes(arrived.at[pl.ds(0, COLS - 1)], part_send)
    wait_bytes(swap_in.at[pl.ds(0, DEVICES - 1)], swap_send)
    for n in range(2):
        wait_bytes(col_in.at[n, pl.ds(0, COLS - 1)], col_send.at[n])
        wait_bytes(row_in.at[n, pl.ds(0, ROWS - 1)], row_send.at[n])


def body(fem_basis, bem_basis, diag, vals, cols, halo, mat, trace, slot):
    fem = jnp.transpose(fem_basis, (0, 2, 1, 3)).reshape(2, VEC, LOCAL)
    bem = jnp.transpose(bem_basis, (0, 2, 1, 3)).reshape(2, VEC, PIECE)
    vmem = pl.BlockSpec(memory_space=pltpu.VMEM)
    dma = pltpu.SemaphoreType.DMA
    next_fem, next_bem, hess, rfac = pl.pallas_call(
        kernel,
        out_shape=(
            jax.ShapeDtypeStruct((2, 16, LOCAL), F32),
            jax.ShapeDtypeStruct((2, 16, PIECE), F32),
            jax.ShapeDtypeStruct((VEC, 16), F32),
            jax.ShapeDtypeStruct((16, 16), F32),
        ),
        in_specs=[vmem] * 6 + [pl.BlockSpec(memory_space=pl.ANY)] + [vmem] * 2,
        out_specs=(vmem,) * 4,
        scratch_shapes=[
            pltpu.VMEM((2, 320, 256), BF16),
            pltpu.VMEM((4, VEC, 128), F32),
            pltpu.VMEM((4, VEC, 128), F32),
            pltpu.VMEM((VEC, ROWS * PIECE), BF16),
            pltpu.VMEM((COLS, VEC, PIECE), F32),
            pltpu.VMEM((COLS, VEC, PIECE), F32),
            pltpu.VMEM((DEVICES, 128), F32),
            pltpu.VMEM((DEVICES, 128), F32),
            pltpu.VMEM((2, 2048, 1024), BF16),
            pltpu.VMEM((VEC, LOCAL), F32),
            pltpu.VMEM((2, 144, WIDE), BF16),
            pltpu.VMEM((48, 128), F32),
            pltpu.VMEM((2, 8, 128), F32),
            pltpu.VMEM((2, COLS, 8, 128), F32),
            pltpu.VMEM((2, ROWS, 8, 128), F32),
            dma((8,)),
            dma((4,)),
            dma((4,)),
            dma, dma, dma, dma, dma, dma,
            dma((2,)), dma((2,)), dma((2,)), dma((2,)),
        ],
        compiler_params=pltpu.CompilerParams(
            has_side_effects=True, vmem_limit_bytes=40 << 20
        ),
    )(fem, bem, diag.reshape(1, LOCAL), vals, cols, halo, mat, trace.reshape(1, 256), slot.reshape(1, PIECE))
    return (
        jnp.transpose(next_fem, (1, 0, 2)),
        jnp.transpose(next_bem, (1, 0, 2)),
        hess.reshape(2, 16, 16),
        rfac,
    )


def solution(mesh):
    both = ("row", "col")
    return jax.shard_map(
        body,
        mesh=mesh,
        in_specs=(
            P(None, None, None, both), P(None, None, None, both), P(both), P(None, both),
            P(None, both), P(None, both), P(None, "row", "col"), P(both), P(both),
        ),
        out_specs=(P(None, None, both), P(None, None, both), P(), P()),
        check_vma=False,
    )
```

```python
import functools

import jax
import jax.numpy as jnp
from jax import lax
from jax.experimental import pallas as pl
from jax.experimental.pallas import tpu as pltpu
from jax.sharding import PartitionSpec as P

F32 = jnp.float32
BF16 = jnp.bfloat16
MESH = pl.DeviceIdType.MESH
HIGHEST = lax.Precision.HIGHEST
ROWS, COLS = 8, 16
DEVICES = ROWS * COLS
VEC = 32
LOCAL = 2048
PIECE = 128
WIDE = LOCAL + PIECE
COUNT = 2.0 * DEVICES * (LOCAL + PIECE)
NT = (((1,), (1,)), ((), ()))
BY_LANE_NEAR = (1, 4, 7, 10, 13)
BY_LANE_FAR = (1, 3, 5, 7, 9, 11, 13)
FIRST_CHUNKS = 4


def split2(x):
    high = x.astype(BF16)
    return high, (x - high.astype(F32)).astype(BF16)


def split3(x):
    high = x.astype(BF16)
    rest = x - high.astype(F32)
    mid = rest.astype(BF16)
    return high, mid, (rest - mid.astype(F32)).astype(BF16)


def lane_gather(table, lanes):
    return jnp.take_along_axis(table, lanes, axis=1, mode="promise_in_bounds")


def small_dot(a, b, dims):
    return lax.dot_general(a, b, (dims, ((), ())), precision=HIGHEST, preferred_element_type=F32)


def looked_up(table, column, tiles, first):
    halves = []
    for half in range(2):
        here = jnp.broadcast_to(column[:, half * 128 : half * 128 + 128], (VEC, 128))
        low = here & 127
        high = here >> 7
        got = jnp.zeros((VEC, 128), F32)
        for t in range(tiles):
            got = jnp.where(high == t + first, lane_gather(table(t), low), got)
        halves.append(got)
    return jnp.concatenate(halves, axis=1)


def multiplied_up(pieces, column, tiles, first):
    low = jnp.broadcast_to((column & 255).astype(jnp.int16), (256, 256))
    high = column >> 8
    hot = jnp.where(
        lax.broadcasted_iota(jnp.int16, (256, 256), 0) == low,
        jnp.ones((256, 256), BF16),
        jnp.zeros((256, 256), BF16),
    )
    found = jnp.dot(pieces, hot, preferred_element_type=F32)
    found = found[: tiles * VEC] + found[tiles * VEC :]
    got = jnp.zeros((VEC, 256), F32)
    for t in range(tiles):
        here = jnp.broadcast_to(high == t + first, (VEC, 256))
        got = jnp.where(here, found[t * VEC : t * VEC + VEC], got)
    return got


def step_kernel(
    fem_hbm, bem_hbm, diag_hbm, vals_hbm, cols_hbm, halo_hbm, mat, trace_hbm, slot_hbm,
    w_hbm, sums,
    fem, bem, diag, vals, cols, halo, trace, slot, in_sem, out_sem,
    near, far, halo_out, halo_in, phi, partial, arrived, swap_out, swap_mid, swap_in,
    mat_buf, image, zp, pack, sum_out, col_in, row_in,
    mat_sem, halo_send, halo_recv, phi_send, phi_recv, part_send, part_recv,
    mid_send, mid_recv, swap_send, swap_recv, col_send, col_recv, row_send, row_recv,
):
    r = lax.axis_index("row")
    c = lax.axis_index("col")

    barrier = pltpu.get_barrier_semaphore()

    def greet_col(k, _):
        there = {"row": r, "col": lax.rem(c + k, COLS)}
        pl.semaphore_signal(barrier, inc=1, device_id=there, device_id_type=MESH)
        return 0

    def greet_row(k, _):
        there = {"row": lax.rem(r + k, ROWS), "col": c}
        pl.semaphore_signal(barrier, inc=1, device_id=there, device_id_type=MESH)
        return 0

    lax.fori_loop(1, ROWS, greet_row, 0)
    lax.fori_loop(1, COLS, greet_col, 0)

    loads = {}

    def load(name, pairs):
        first = 4 * len(loads)
        loads[name] = [
            pltpu.make_async_copy(a, b, in_sem.at[first + i]) for i, (a, b) in enumerate(pairs)
        ]
        for copy in loads[name]:
            copy.start()

    def ready(*names):
        for name in names:
            for copy in loads[name]:
                copy.wait()

    def parts(whole, held, blocks):
        return [
            (whole.at[b, :, p, :], held.at[b, pl.ds(p * 16, 16), :])
            for b in blocks
            for p in range(2)
        ]

    load("bem", parts(bem_hbm, bem, (0, 1)))
    load("fem", parts(fem_hbm, fem, (1,)))
    load("index", [(halo_hbm, halo), (trace_hbm, trace), (slot_hbm, slot)])
    load("sparse", [(cols_hbm, cols), (vals_hbm, vals), (diag_hbm, diag)])
    load("old", parts(fem_hbm, fem, (0,)))

    def matrix_copy(k):
        chunk = lax.rem(k + c // 2, 8)
        rows = pl.ds(pl.multiple_of(chunk * 256, 256), 256)
        return pltpu.make_async_copy(mat.at[:, rows, :], mat_buf.at[:, rows, :], mat_sem.at[k])

    for k in range(8):
        matrix_copy(k).start()

    def remote(src, dst, send, recv, row, col):
        return pltpu.make_async_remote_copy(
            src_ref=src, dst_ref=dst, send_sem=send, recv_sem=recv,
            device_id={"row": row, "col": col}, device_id_type=MESH,
        )

    def wait_bytes(ref, sem):
        pltpu.make_async_copy(ref, ref, sem).wait()

    ready("bem")
    mine = pl.ds(pl.multiple_of(r * PIECE, PIECE), PIECE)
    phi[:, mine] = bem[1].astype(BF16)

    ready("index", "fem")

    def picked(rows):
        rows = jnp.broadcast_to(rows, (VEC, 128))
        high = rows >> 7
        low = rows & 127
        out = jnp.zeros((VEC, 128), F32)
        for t in range(LOCAL // 128):
            out = jnp.where(high == t, lane_gather(fem[1, :, t * 128 : (t + 1) * 128], low), out)
        return out

    for d in range(4):
        halo_out[d] = picked(halo[d : d + 1, :])
    for d, missing in enumerate((c == 0, c == COLS - 1, r == 0, r == ROWS - 1)):

        @pl.when(missing)
        def _(d=d):
            halo_in[d] = jnp.zeros((VEC, 128), F32)

    lane = lax.broadcasted_iota(jnp.int32, (8, 128), 1)
    trace_lo = jnp.broadcast_to(trace[:, :128], (8, 128))
    trace_hi = jnp.broadcast_to(trace[:, 128:], (8, 128))
    trace_q = []
    for q in range(2):
        source = (2 * lane + q) & 127
        full = jnp.where(lane < 64, lane_gather(trace_lo, source), lane_gather(trace_hi, source))
        trace_q.append(full[:1])
    leaving = [picked(jnp.maximum(t, 0)) * (t >= 0).astype(F32) for t in trace_q]
    owner = lax.broadcasted_iota(jnp.int32, (2 * DEVICES, PIECE), 0)
    owner = jnp.where(owner < DEVICES, 2 * owner, 2 * (owner - DEVICES) + 1)
    places = (owner == slot[...]).astype(F32).astype(BF16)
    back = lax.dot_general(
        jnp.concatenate(split3(bem[1]), axis=0), places, NT, preferred_element_type=F32
    )
    back = back[:VEC] + back[VEC : 2 * VEC] + back[2 * VEC :]
    swap_out[...] = jnp.concatenate(leaving + [back[:, :128], back[:, 128:]], axis=0).T

    for t in range(8):
        for a, piece in enumerate(split2(fem[1, :, t * 256 : (t + 1) * 256])):
            near[a * 256 + t * 32 : a * 256 + t * 32 + 32, :] = piece
    ready("sparse")

    def product_near(j, _):
        here = pl.ds(pl.multiple_of(j * 256, 256), 256)
        acc = diag[:, here] * fem[1, :, here]
        for k in range(16):
            column = cols[k : k + 1, here]
            if k in BY_LANE_NEAR:
                got = looked_up(lambda t: fem[1, :, t * 128 : (t + 1) * 128], column, 16, 0)
            else:
                got = multiplied_up(near[...], column, 8, 0)
            acc = acc + vals[k : k + 1, here] * got
        image[:, here] = acc
        return 0

    lax.fori_loop(0, FIRST_CHUNKS, product_near, 0)

    pl.semaphore_wait(barrier, ROWS + COLS - 2)

    def send_phi(k, _):
        other = lax.rem(r + k, ROWS)
        remote(phi.at[:, mine], phi.at[:, mine], phi_send, phi_recv, other, c).start()
        return 0

    lax.fori_loop(1, ROWS, send_phi, 0)

    neighbours = (
        (c + 1 < COLS, r, c + 1, c > 0),
        (c > 0, r, c - 1, c + 1 < COLS),
        (r + 1 < ROWS, r + 1, c, r > 0),
        (r > 0, r - 1, c, r + 1 < ROWS),
    )
    for d, (exists, row, col, _) in enumerate(neighbours):

        @pl.when(exists)
        def _(d=d, row=row, col=col):
            remote(
                halo_out.at[d], halo_in.at[d], halo_send.at[d], halo_recv.at[d], row, col
            ).start()

    def send_mid(k, _):
        other = lax.rem(r + k, ROWS)
        block = pl.ds(pl.multiple_of(other * COLS, COLS), COLS)
        remote(swap_out.at[block], swap_mid.at[r], mid_send, mid_recv, other, c).start()
        return 0

    lax.fori_loop(1, ROWS, send_mid, 0)
    swap_mid[r] = swap_out[pl.ds(pl.multiple_of(r * COLS, COLS), COLS)]

    lax.fori_loop(FIRST_CHUNKS, LOCAL // 256, product_near, 0)

    wait_bytes(phi.at[:, pl.ds(0, (ROWS - 1) * PIECE)], phi_recv)
    phi_all = phi[...]
    turned = jnp.concatenate([-phi_all[16:], phi_all[:16]], axis=0)

    def multiply(k, _):
        chunk = lax.rem(k + c // 2, 8)
        matrix_copy(k).wait()
        rows = pl.ds(pl.multiple_of(chunk * 256, 256), 256)
        out = lax.dot_general(phi_all, mat_buf[0, rows, :], NT, preferred_element_type=F32)
        out = out + lax.dot_general(turned, mat_buf[1, rows, :], NT, preferred_element_type=F32)
        for half in range(2):
            other = 2 * chunk + half
            partial[other] = out[:, half * 128 : half * 128 + 128]

            @pl.when(other != c)
            def _():
                remote(partial.at[other], arrived.at[c], part_send, part_recv, r, other).start()

        return 0

    lax.fori_loop(0, 8, multiply, 0)
    arrived[c] = partial[c]

    wait_bytes(swap_mid.at[pl.ds(0, ROWS - 1)], mid_recv)

    def send_swap(k, _):
        other = lax.rem(c + k, COLS)
        remote(
            swap_mid.at[:, pl.ds(other, 1), :], swap_in.at[:, pl.ds(c, 1), :],
            swap_send, swap_recv, r, other,
        ).start()
        return 0

    lax.fori_loop(1, COLS, send_swap, 0)
    swap_in[:, pl.ds(c, 1), :] = swap_mid[:, pl.ds(c, 1), :]

    ready("old")
    for p in range(2):
        for b in range(2):
            rows = slice(p * 16, p * 16 + 16)
            for a, x in enumerate(split3(fem[b, rows, :])):
                zp[p, a * 48 + b * 16 : a * 48 + b * 16 + 16, :LOCAL] = x
            for a, x in enumerate(split3(bem[b, rows, :])):
                zp[p, a * 48 + b * 16 : a * 48 + b * 16 + 16, LOCAL:] = x
    own = jnp.zeros((VEC, VEC), F32)
    for p in range(2):
        whole = jnp.concatenate([zp[p, a * 48 : a * 48 + 32, :] for a in range(3)], axis=0)
        for b in range(3):
            both = lax.dot_general(
                whole, zp[p, b * 48 : b * 48 + 32, :], NT, preferred_element_type=F32
            )
            own = own + both[:32] + both[32:64] + both[64:]
    pack[...] = jnp.zeros((48, 128), F32)
    pack[:32, :32] = own
    packed = pack[0:8, :]
    for g in range(1, 4):
        packed = packed + pltpu.roll(pack[8 * g : 8 * g + 8, :], 32 * g, 1)
    sum_out[0] = packed

    def reduce_cols(n):
        col_in[n, c] = sum_out[n]

        def send(k, _):
            other = lax.rem(c + k, COLS)
            remote(sum_out.at[n], col_in.at[n, c], col_send.at[n], col_recv.at[n], r, other).start()
            return 0

        lax.fori_loop(1, COLS, send, 0)

    def reduce_rows(n):
        wait_bytes(col_in.at[n, pl.ds(0, COLS - 1)], col_recv.at[n])
        total = col_in[n, 0]
        for k in range(1, COLS):
            total = total + col_in[n, k]
        row_in[n, r] = total

        def send(k, _):
            other = lax.rem(r + k, ROWS)
            remote(row_in.at[n, r], row_in.at[n, r], row_send.at[n], row_recv.at[n], other, c).start()
            return 0

        lax.fori_loop(1, ROWS, send, 0)

    def reduced(n):
        wait_bytes(row_in.at[n, pl.ds(0, ROWS - 1)], row_recv.at[n])
        total = row_in[n, 0]
        for k in range(1, ROWS):
            total = total + row_in[n, k]
        return total * (1.0 / COUNT)

    reduce_cols(0)

    for d, (_, _, _, comes) in enumerate(neighbours):

        @pl.when(comes)
        def _(d=d):
            wait_bytes(halo_in.at[d], halo_recv.at[d])

    for t in range(2):
        x = jnp.concatenate([halo_in[2 * t], halo_in[2 * t + 1]], axis=1)
        for a, piece in enumerate(split2(x)):
            far[a * 64 + t * 32 : a * 64 + t * 32 + 32, :] = piece

    def product_far(j, _):
        here = pl.ds(pl.multiple_of(j * 256, 256), 256)
        acc = image[:, here]
        for k in range(16):
            column = cols[k : k + 1, here]
            if k in BY_LANE_FAR:
                got = looked_up(lambda t: halo_in[t], column, 4, 16)
            else:
                got = multiplied_up(far[...], column, 2, 8)
            acc = acc + vals[k : k + 1, here] * got
        image[:, here] = acc
        return 0

    lax.fori_loop(0, LOCAL // 256, product_far, 0)
    reduce_rows(0)

    wait_bytes(swap_in.at[:, pl.ds(0, COLS - 1), :], swap_recv)
    met = swap_in[...].reshape(DEVICES, 128).T
    chosen = jnp.broadcast_to(slot[...], (VEC, PIECE))
    taken = jnp.where(
        (chosen & 1) == 0, lane_gather(met[:32], chosen >> 1), lane_gather(met[32:64], chosen >> 1)
    )
    answers = jnp.concatenate([met[64:96], met[96:]], axis=1)
    answers = jnp.concatenate(split3(answers), axis=0)
    targets = jnp.concatenate(trace_q, axis=1)
    for t in range(LOCAL // 256):
        row = lax.broadcasted_iota(jnp.int32, (256, 256), 0) + t * 256
        hot = (row == targets).astype(F32).astype(BF16)
        put = lax.dot_general(answers, hot, NT, preferred_element_type=F32)
        here = slice(t * 256, t * 256 + 256)
        image[:, here] = image[:, here] + put[:32] + put[32:64] + put[64:]
    for p in range(2):
        for a, x in enumerate(split3(image[p * 16 : p * 16 + 16, :LOCAL])):
            zp[p, a * 48 + 32 : a * 48 + 48, :LOCAL] = x

    def inner(columns):
        made = jnp.zeros((48, 16), F32)
        for p in range(2):
            whole = zp[p, :, columns]
            for b in range(3):
                both = lax.dot_general(
                    whole, zp[p, b * 48 + 32 : b * 48 + 48, columns], NT,
                    preferred_element_type=F32,
                )
                made = made + both[:48] + both[48:96] + both[96:]
        return made

    pack[...] = jnp.zeros((48, 128), F32)
    pack[:, :16] = inner(slice(0, LOCAL))
    wait_bytes(arrived.at[pl.ds(0, COLS - 1)], part_recv)
    bem_image = taken
    for k in range(COLS):
        bem_image = bem_image + arrived[k]
    image[:, LOCAL:] = bem_image
    for p in range(2):
        for a, x in enumerate(split3(bem_image[p * 16 : p * 16 + 16, :])):
            zp[p, a * 48 + 32 : a * 48 + 48, LOCAL:] = x
    pack[:, :16] = pack[:, :16] + inner(slice(LOCAL, WIDE))
    packed = pack[0:8, :]
    for g in range(1, 6):
        packed = packed + pltpu.roll(pack[8 * g : 8 * g + 8, :], 16 * g, 1)
    sum_out[1] = packed
    reduce_cols(1)
    leave = pltpu.make_async_copy(image, w_hbm, out_sem)
    leave.start()
    sums[:8, :] = reduced(0)

    for d, (exists, _, _, _) in enumerate(neighbours):

        @pl.when(exists)
        def _(d=d):
            wait_bytes(halo_out.at[d], halo_send.at[d])

    wait_bytes(phi.at[:, pl.ds(0, (ROWS - 1) * PIECE)], phi_send)
    wait_bytes(arrived.at[pl.ds(0, COLS - 1)], part_send)
    wait_bytes(swap_mid.at[pl.ds(0, ROWS - 1)], mid_send)
    wait_bytes(swap_in.at[:, pl.ds(0, COLS - 1), :], swap_send)
    wait_bytes(col_in.at[0, pl.ds(0, COLS - 1)], col_send.at[0])
    wait_bytes(row_in.at[0, pl.ds(0, ROWS - 1)], row_send.at[0])
    reduce_rows(1)
    wait_bytes(col_in.at[1, pl.ds(0, COLS - 1)], col_send.at[1])
    leave.wait()
    sums[8:, :] = reduced(1)
    wait_bytes(row_in.at[1, pl.ds(0, ROWS - 1)], row_send.at[1])


def finish_kernel(
    fem_hbm, bem_hbm, w_hbm, sums, next_fem, next_bem, hess, rfac,
    basis, image, pack_q, pack, fem_out, bem_out, in_sem, out_sem,
):
    copies = []
    for b in range(2):
        for p in range(2):
            rows = pl.ds(b * 16, 16)
            copies.append((fem_hbm.at[b, :, p, :], basis.at[p, rows, pl.ds(0, LOCAL)]))
            copies.append((bem_hbm.at[b, :, p, :], basis.at[p, rows, pl.ds(LOCAL, PIECE)]))
    copies.append((w_hbm, image))
    copies = [pltpu.make_async_copy(a, b, in_sem.at[i]) for i, (a, b) in enumerate(copies)]
    for copy in copies:
        copy.start()

    total = sums[:8, :]
    for g in range(4):
        pack_q[8 * g : 8 * g + 8, :] = total if g == 0 else pltpu.roll(total, 128 - 32 * g, 1)
    gram_q = pack_q[:, :32]
    total = sums[8:, :]
    for g in range(6):
        pack[8 * g : 8 * g + 8, :] = total if g == 0 else pltpu.roll(total, 128 - 16 * g, 1)
    one = pack[:32, :16]
    norm = pack[32:48, :16]

    both = 2.0 * one - small_dot(gram_q, one, ((1,), (0,)))
    hess[...] = both
    left = small_dot(gram_q, both, ((1,), (0,))) - one
    gram = norm + small_dot(both, left, ((0,), (0,))) - small_dot(one, both, ((0,), (0,)))
    row_id = lax.broadcasted_iota(jnp.int32, (16, 16), 0)
    col_id = lax.broadcasted_iota(jnp.int32, (16, 16), 1)
    work = (gram + gram.T) * 0.5
    inverse = (row_id == col_id).astype(F32)
    upper = jnp.zeros((16, 16), F32)
    lower_inv = jnp.zeros((16, 16), F32)
    for j in range(16):
        pivot = work[j : j + 1, j : j + 1]
        root = lax.rsqrt(pivot)
        root = root * (1.5 - 0.5 * pivot * root * root)
        line = jnp.broadcast_to(work[j : j + 1, :] * root, (16, 16))
        line_inv = jnp.broadcast_to(inverse[j : j + 1, :] * root, (16, 16))
        column = jnp.broadcast_to(work[:, j : j + 1] * root, (16, 16))
        upper = jnp.where((row_id == j) & (col_id >= j), line, upper)
        lower_inv = jnp.where(row_id == j, line_inv, lower_inv)
        work = work - column * line
        inverse = inverse - column * line_inv
    rfac[...] = upper

    weights = -small_dot(lower_inv, both, ((1,), (1,)))
    w_pair = jnp.concatenate(split2(weights), axis=0)
    l_pair = jnp.concatenate(split2(lower_inv), axis=0)
    for copy in copies:
        copy.wait()
    leaving = []
    for p in range(2):
        q_high, q_low = split2(basis[p])
        i_high, i_low = split2(image[p * 16 : p * 16 + 16, :])
        first = jnp.dot(w_pair, q_high, preferred_element_type=F32)
        first = first + jnp.dot(l_pair, i_high, preferred_element_type=F32)
        second = jnp.dot(w_pair[:16], q_low, preferred_element_type=F32)
        second = second + jnp.dot(l_pair[:16], i_low, preferred_element_type=F32)
        made = first[:16] + first[16:] + second
        fem_out[p] = made[:, :LOCAL]
        bem_out[p] = made[:, LOCAL:]
        leaving.append(pltpu.make_async_copy(fem_out.at[p], next_fem.at[:, p, :], out_sem.at[p]))
        leaving.append(
            pltpu.make_async_copy(bem_out.at[p], next_bem.at[:, p, :], out_sem.at[2 + p])
        )
        leaving[-2].start()
        leaving[-1].start()
    for copy in leaving:
        copy.wait()


def body(fem_basis, bem_basis, diag, vals, cols, halo, mat, trace, slot):
    vmem = pl.BlockSpec(memory_space=pltpu.VMEM)
    hbm = pl.BlockSpec(memory_space=pl.ANY)
    dma = pltpu.SemaphoreType.DMA
    image, sums = pl.pallas_call(
        step_kernel,
        out_shape=(
            jax.ShapeDtypeStruct((VEC, WIDE), F32),
            jax.ShapeDtypeStruct((16, 128), F32),
        ),
        in_specs=[hbm] * 9,
        out_specs=(hbm, vmem),
        scratch_shapes=[
            pltpu.VMEM((2, VEC, LOCAL), F32),
            pltpu.VMEM((2, VEC, PIECE), F32),
            pltpu.VMEM((1, LOCAL), F32),
            pltpu.VMEM((16, LOCAL), F32),
            pltpu.VMEM((16, LOCAL), jnp.int32),
            pltpu.VMEM((4, 128), jnp.int32),
            pltpu.VMEM((1, 256), jnp.int32),
            pltpu.VMEM((1, PIECE), jnp.int32),
            dma((20,)),
            dma,
            pltpu.VMEM((512, 256), BF16),
            pltpu.VMEM((128, 256), BF16),
            pltpu.VMEM((4, VEC, 128), F32),
            pltpu.VMEM((4, VEC, 128), F32),
            pltpu.VMEM((VEC, ROWS * PIECE), BF16),
            pltpu.VMEM((COLS, VEC, PIECE), F32),
            pltpu.VMEM((COLS, VEC, PIECE), F32),
            pltpu.VMEM((DEVICES, 128), F32),
            pltpu.VMEM((ROWS, COLS, 128), F32),
            pltpu.VMEM((ROWS, COLS, 128), F32),
            pltpu.VMEM((2, 2048, 1024), BF16),
            pltpu.VMEM((VEC, WIDE), F32),
            pltpu.VMEM((2, 144, WIDE), BF16),
            pltpu.VMEM((48, 128), F32),
            pltpu.VMEM((2, 8, 128), F32),
            pltpu.VMEM((2, COLS, 8, 128), F32),
            pltpu.VMEM((2, ROWS, 8, 128), F32),
            dma((8,)),
            dma((4,)),
            dma((4,)),
            dma, dma, dma, dma, dma, dma, dma, dma,
            dma((2,)), dma((2,)), dma((2,)), dma((2,)),
        ],
        compiler_params=pltpu.CompilerParams(
            has_side_effects=True, collective_id=0, vmem_limit_bytes=60 << 20
        ),
    )(fem_basis, bem_basis, diag.reshape(1, LOCAL), vals, cols, halo, mat, trace.reshape(1, 256), slot.reshape(1, PIECE))
    next_fem, next_bem, hess, rfac = pl.pallas_call(
        finish_kernel,
        out_shape=(
            jax.ShapeDtypeStruct((16, 2, LOCAL), F32),
            jax.ShapeDtypeStruct((16, 2, PIECE), F32),
            jax.ShapeDtypeStruct((VEC, 16), F32),
            jax.ShapeDtypeStruct((16, 16), F32),
        ),
        in_specs=[hbm, hbm, hbm, vmem],
        out_specs=(hbm, hbm, vmem, vmem),
        scratch_shapes=[
            pltpu.VMEM((2, VEC, WIDE), F32),
            pltpu.VMEM((VEC, WIDE), F32),
            pltpu.VMEM((VEC, 128), F32),
            pltpu.VMEM((48, 128), F32),
            pltpu.VMEM((2, 16, LOCAL), F32),
            pltpu.VMEM((2, 16, PIECE), F32),
            dma((9,)),
            dma((4,)),
        ],
        compiler_params=pltpu.CompilerParams(vmem_limit_bytes=60 << 20),
    )(fem_basis, bem_basis, image, sums)
    return next_fem, next_bem, hess.reshape(2, 16, 16), rfac


def solution(mesh):
    both = ("row", "col")
    return jax.shard_map(
        body,
        mesh=mesh,
        in_specs=(
            P(None, None, None, both), P(None, None, None, both), P(both), P(None, both),
            P(None, both), P(None, both), P(None, "row", "col"), P(both), P(both),
        ),
        out_specs=(P(None, None, both), P(None, None, both), P(), P()),
        check_vma=False,
    )
```

```python
import functools

import jax
import jax.numpy as jnp
from jax import lax
from jax.experimental import pallas as pl
from jax.experimental.pallas import tpu as pltpu
from jax.sharding import PartitionSpec as P

F32 = jnp.float32
BF16 = jnp.bfloat16
MESH = pl.DeviceIdType.MESH
HIGHEST = lax.Precision.HIGHEST
ROWS, COLS = 8, 16
DEVICES = ROWS * COLS
VEC = 32
LOCAL = 2048
PIECE = 128
WIDE = LOCAL + PIECE
COUNT = 2.0 * DEVICES * (LOCAL + PIECE)
NT = (((1,), (1,)), ((), ()))
BY_LANE_NEAR = (1, 3, 5, 7, 9, 11, 13, 15)
BY_LANE_FAR = (1, 3, 5, 7, 9, 11, 13, 15)
BY_LANE_ALL = (1, 3, 5, 7, 9, 11, 13, 15)
FIRST_CHUNKS = 4


def split2(x):
    high = x.astype(BF16)
    return high, (x - high.astype(F32)).astype(BF16)


def split3(x):
    high = x.astype(BF16)
    rest = x - high.astype(F32)
    mid = rest.astype(BF16)
    return high, mid, (rest - mid.astype(F32)).astype(BF16)


def lane_gather(table, lanes):
    return jnp.take_along_axis(table, lanes, axis=1, mode="promise_in_bounds")


def small_dot(a, b, dims):
    return lax.dot_general(a, b, (dims, ((), ())), precision=HIGHEST, preferred_element_type=F32)


def paired(x):
    top = jnp.maximum(jnp.max(jnp.abs(x), axis=1, keepdims=True), 1e-30)
    whole = jnp.round(x * (32000.0 / top)).astype(jnp.int32)
    return (whole[:16] << 16) | (whole[16:] & 0xFFFF), top * (1.0 / 32000.0)


def looked_up(table, column, tiles, first):
    halves = []
    for half in range(2):
        here = jnp.broadcast_to(column[:, half * 128 : half * 128 + 128], (16, 128))
        low = here & 127
        high = here >> 7
        got = jnp.zeros((16, 128), jnp.int32)
        for t in range(tiles):
            got = jnp.where(high == t + first, lane_gather(table(t), low), got)
        halves.append(got)
    got = jnp.concatenate(halves, axis=1)
    return jnp.concatenate([got >> 16, (got << 16) >> 16], axis=0).astype(F32)


def multiplied_up(pieces, column, tiles, first):
    low = jnp.broadcast_to((column & 255).astype(jnp.int16), (256, 256))
    high = column >> 8
    hot = jnp.where(
        lax.broadcasted_iota(jnp.int16, (256, 256), 0) == low,
        jnp.ones((256, 256), BF16),
        jnp.zeros((256, 256), BF16),
    )
    found = jnp.dot(pieces, hot, preferred_element_type=F32)
    found = found[: tiles * VEC] + found[tiles * VEC :]
    got = jnp.zeros((VEC, 256), F32)
    for t in range(tiles):
        here = jnp.broadcast_to(high == t + first, (VEC, 256))
        got = jnp.where(here, found[t * VEC : t * VEC + VEC], got)
    return got


def step_kernel(
    fem_hbm, bem_hbm, diag_hbm, vals_hbm, cols_hbm, halo_hbm, mat, trace_hbm, slot_hbm,
    w_hbm, sums,
    fem, bem, diag, vals, cols, halo, trace, slot, in_sem, out_sem,
    near, pairs, unit, halo_out, halo_in, phi, partial, arrived, swap_out, swap_mid, swap_in,
    mat_buf, image, zp, pack, sum_out, col_in, row_in,
    mat_sem, halo_send, halo_recv, phi_send, phi_recv, part_send, part_recv,
    mid_send, mid_recv, swap_send, swap_recv, col_send, col_recv, row_send, row_recv,
):
    r = lax.axis_index("row")
    c = lax.axis_index("col")

    barrier = pltpu.get_barrier_semaphore()

    def greet_col(k, _):
        there = {"row": r, "col": lax.rem(c + k, COLS)}
        pl.semaphore_signal(barrier, inc=1, device_id=there, device_id_type=MESH)
        return 0

    def greet_row(k, _):
        there = {"row": lax.rem(r + k, ROWS), "col": c}
        pl.semaphore_signal(barrier, inc=1, device_id=there, device_id_type=MESH)
        return 0

    lax.fori_loop(1, ROWS, greet_row, 0)
    lax.fori_loop(1, COLS, greet_col, 0)

    loads = {}

    def load(name, pairs):
        first = 4 * len(loads)
        loads[name] = [
            pltpu.make_async_copy(a, b, in_sem.at[first + i]) for i, (a, b) in enumerate(pairs)
        ]
        for copy in loads[name]:
            copy.start()

    def ready(*names):
        for name in names:
            for copy in loads[name]:
                copy.wait()

    def parts(whole, held, blocks):
        return [
            (whole.at[b, :, p, :], held.at[b, pl.ds(p * 16, 16), :])
            for b in blocks
            for p in range(2)
        ]

    load("bem", parts(bem_hbm, bem, (0, 1)))
    load("fem", parts(fem_hbm, fem, (1,)))
    load("index", [(halo_hbm, halo), (trace_hbm, trace), (slot_hbm, slot)])
    load("sparse", [(cols_hbm, cols), (vals_hbm, vals), (diag_hbm, diag)])
    load("old", parts(fem_hbm, fem, (0,)))

    def matrix_copy(k):
        chunk = lax.rem(k + c // 2, 8)
        rows = pl.ds(pl.multiple_of(chunk * 256, 256), 256)
        return pltpu.make_async_copy(mat.at[:, rows, :], mat_buf.at[:, rows, :], mat_sem.at[k])

    for k in range(8):
        matrix_copy(k).start()

    def remote(src, dst, send, recv, row, col):
        return pltpu.make_async_remote_copy(
            src_ref=src, dst_ref=dst, send_sem=send, recv_sem=recv,
            device_id={"row": row, "col": col}, device_id_type=MESH,
        )

    def wait_bytes(ref, sem):
        pltpu.make_async_copy(ref, ref, sem).wait()

    ready("bem")
    mine = pl.ds(pl.multiple_of(r * PIECE, PIECE), PIECE)
    phi[:, mine] = bem[1].astype(BF16)

    ready("index", "fem")

    def picked(rows):
        rows = jnp.broadcast_to(rows, (VEC, 128))
        high = rows >> 7
        low = rows & 127
        out = jnp.zeros((VEC, 128), F32)
        for t in range(LOCAL // 128):
            out = jnp.where(high == t, lane_gather(fem[1, :, t * 128 : (t + 1) * 128], low), out)
        return out

    for d in range(4):
        halo_out[d] = picked(halo[d : d + 1, :])
    for d, missing in enumerate((c == 0, c == COLS - 1, r == 0, r == ROWS - 1)):

        @pl.when(missing)
        def _(d=d):
            halo_in[d] = jnp.zeros((VEC, 128), F32)

    pl.semaphore_wait(barrier, ROWS + COLS - 2)

    def send_phi(k, _):
        other = lax.rem(r + k, ROWS)
        remote(phi.at[:, mine], phi.at[:, mine], phi_send, phi_recv, other, c).start()
        return 0

    lax.fori_loop(1, ROWS, send_phi, 0)

    neighbours = (
        (c + 1 < COLS, r, c + 1, c > 0),
        (c > 0, r, c - 1, c + 1 < COLS),
        (r + 1 < ROWS, r + 1, c, r > 0),
        (r > 0, r - 1, c, r + 1 < ROWS),
    )
    for d, (exists, row, col, _) in enumerate(neighbours):

        @pl.when(exists)
        def _(d=d, row=row, col=col):
            remote(
                halo_out.at[d], halo_in.at[d], halo_send.at[d], halo_recv.at[d], row, col
            ).start()

    lane = lax.broadcasted_iota(jnp.int32, (8, 128), 1)
    trace_lo = jnp.broadcast_to(trace[:, :128], (8, 128))
    trace_hi = jnp.broadcast_to(trace[:, 128:], (8, 128))
    trace_q = []
    for q in range(2):
        source = (2 * lane + q) & 127
        full = jnp.where(lane < 64, lane_gather(trace_lo, source), lane_gather(trace_hi, source))
        trace_q.append(full[:1])
    leaving = [picked(jnp.maximum(t, 0)) * (t >= 0).astype(F32) for t in trace_q]
    owner = lax.broadcasted_iota(jnp.int32, (2 * DEVICES, PIECE), 0)
    owner = jnp.where(owner < DEVICES, 2 * owner, 2 * (owner - DEVICES) + 1)
    places = (owner == slot[...]).astype(F32).astype(BF16)
    back = lax.dot_general(
        jnp.concatenate(split3(bem[1]), axis=0), places, NT, preferred_element_type=F32
    )
    back = back[:VEC] + back[VEC : 2 * VEC] + back[2 * VEC :]
    swap_out[...] = jnp.concatenate(leaving + [back[:, :128], back[:, 128:]], axis=0).T

    def send_mid(k, _):
        other = lax.rem(r + k, ROWS)
        block = pl.ds(pl.multiple_of(other * COLS, COLS), COLS)
        remote(swap_out.at[block], swap_mid.at[r], mid_send, mid_recv, other, c).start()
        return 0

    lax.fori_loop(1, ROWS, send_mid, 0)
    swap_mid[r] = swap_out[pl.ds(pl.multiple_of(r * COLS, COLS), COLS)]

    ready("old")
    for p in range(2):
        rows = slice(p * 16, p * 16 + 16)
        for b in range(2):
            for a, x in enumerate(split2(fem[b, rows, :])):
                zp[p, a * 48 + b * 16 : a * 48 + b * 16 + 16, :LOCAL] = x
            for a, x in enumerate(split2(bem[b, rows, :])):
                zp[p, a * 48 + b * 16 : a * 48 + b * 16 + 16, LOCAL:] = x
    own = jnp.zeros((VEC, VEC), F32)
    for p in range(2):
        whole = jnp.concatenate([zp[p, :32, :], zp[p, 48:80, :]], axis=0)
        for b in range(2):
            both = lax.dot_general(
                whole, zp[p, b * 48 : b * 48 + 32, :], NT, preferred_element_type=F32
            )
            own = own + both[:32] + both[32:]
    pack[...] = jnp.zeros((48, 128), F32)
    pack[:32, :32] = own
    packed = pack[0:8, :]
    for g in range(1, 4):
        packed = packed + pltpu.roll(pack[8 * g : 8 * g + 8, :], 32 * g, 1)
    sum_out[8:, :] = packed

    for t in range(8):
        for a, piece in enumerate(split2(fem[1, :, t * 256 : (t + 1) * 256])):
            near[a * 320 + t * 32 : a * 320 + t * 32 + 32, :] = piece
    pairs[:, :LOCAL], unit[...] = paired(fem[1])
    ready("sparse")

    def product(j, where, tiles, first, by_lane, start):
        here = pl.ds(pl.multiple_of(j * 256, 256), 256)
        acc = start(here)
        lane_acc = jnp.zeros((VEC, 256), F32)
        high = where[first * VEC : (first + tiles) * VEC, :]
        low = where[(10 + first) * VEC : (10 + first + tiles) * VEC, :]
        pieces = jnp.concatenate([high, low], axis=0)
        for k in range(16):
            column = cols[k : k + 1, here]
            value = vals[k : k + 1, here]
            if k in by_lane:
                got = looked_up(
                    lambda t: pairs[:, (2 * first + t) * 128 : (2 * first + t + 1) * 128],
                    column, 2 * tiles, 2 * first,
                )
                lane_acc = lane_acc + value * got
            else:
                acc = acc + value * multiplied_up(pieces, column, tiles, first)
        image[:, here] = acc + lane_acc * unit[...]
        return 0

    def diagonal(here):
        return diag[:, here] * fem[1, :, here]

    def product_near(j, _):
        return product(j, near, 8, 0, BY_LANE_NEAR, diagonal)

    def product_far(j, _):
        return product(j, near, 2, 8, BY_LANE_FAR, lambda here: image[:, here])

    def product_all(j, _):
        return product(j, near, 10, 0, BY_LANE_ALL, diagonal)

    lax.fori_loop(0, FIRST_CHUNKS, product_near, 0)

    wait_bytes(swap_mid.at[pl.ds(0, ROWS - 1)], mid_recv)

    def send_swap(k, _):
        other = lax.rem(c + k, COLS)
        remote(
            swap_mid.at[:, pl.ds(other, 1), :], swap_in.at[:, pl.ds(c, 1), :],
            swap_send, swap_recv, r, other,
        ).start()
        return 0

    lax.fori_loop(1, COLS, send_swap, 0)
    swap_in[:, pl.ds(c, 1), :] = swap_mid[:, pl.ds(c, 1), :]

    wait_bytes(phi.at[:, pl.ds(0, (ROWS - 1) * PIECE)], phi_recv)
    phi_all = phi[...]
    turned = jnp.concatenate([-phi_all[16:], phi_all[:16]], axis=0)

    def multiply(k, _):
        chunk = lax.rem(k + c // 2, 8)
        matrix_copy(k).wait()
        rows = pl.ds(pl.multiple_of(chunk * 256, 256), 256)
        out = lax.dot_general(phi_all, mat_buf[0, rows, :], NT, preferred_element_type=F32)
        out = out + lax.dot_general(turned, mat_buf[1, rows, :], NT, preferred_element_type=F32)
        for half in range(2):
            other = 2 * chunk + half
            partial[other] = out[:, half * 128 : half * 128 + 128]

            @pl.when(other != c)
            def _():
                remote(partial.at[other], arrived.at[c], part_send, part_recv, r, other).start()

        return 0

    lax.fori_loop(0, 8, multiply, 0)
    arrived[c] = partial[c]

    def reduce_cols():
        col_in[c] = sum_out[...]

        def send(k, _):
            other = lax.rem(c + k, COLS)
            remote(sum_out, col_in.at[c], col_send, col_recv, r, other).start()
            return 0

        lax.fori_loop(1, COLS, send, 0)

    def reduce_rows():
        wait_bytes(col_in.at[pl.ds(0, COLS - 1)], col_recv)
        total = col_in[0]
        for k in range(1, COLS):
            total = total + col_in[k]
        row_in[r] = total

        def send(k, _):
            other = lax.rem(r + k, ROWS)
            remote(row_in.at[r], row_in.at[r], row_send, row_recv, other, c).start()
            return 0

        lax.fori_loop(1, ROWS, send, 0)

    def reduced():
        wait_bytes(row_in.at[pl.ds(0, ROWS - 1)], row_recv)
        total = row_in[0]
        for k in range(1, ROWS):
            total = total + row_in[k]
        return total * (1.0 / COUNT)

    for d, (_, _, _, comes) in enumerate(neighbours):

        @pl.when(comes)
        def _(d=d):
            wait_bytes(halo_in.at[d], halo_recv.at[d])

    outer = jnp.concatenate([halo_in[d] for d in range(4)], axis=1)
    for t in range(2):
        for a, piece in enumerate(split2(outer[:, t * 256 : t * 256 + 256])):
            near[a * 320 + 256 + t * 32 : a * 320 + 288 + t * 32, :] = piece
    pairs[...], unit[...] = paired(jnp.concatenate([fem[1], outer], axis=1))
    lax.fori_loop(0, FIRST_CHUNKS, product_far, 0)
    lax.fori_loop(FIRST_CHUNKS, LOCAL // 256, product_all, 0)

    wait_bytes(swap_in.at[:, pl.ds(0, COLS - 1), :], swap_recv)
    met = swap_in[...].reshape(DEVICES, 128).T
    chosen = jnp.broadcast_to(slot[...], (VEC, PIECE))
    taken = jnp.where(
        (chosen & 1) == 0, lane_gather(met[:32], chosen >> 1), lane_gather(met[32:64], chosen >> 1)
    )
    answers = jnp.concatenate([met[64:96], met[96:]], axis=1)
    answers = jnp.concatenate(split3(answers), axis=0)
    targets = jnp.concatenate(trace_q, axis=1)
    for t in range(LOCAL // 256):
        row = lax.broadcasted_iota(jnp.int32, (256, 256), 0) + t * 256
        hot = (row == targets).astype(F32).astype(BF16)
        put = lax.dot_general(answers, hot, NT, preferred_element_type=F32)
        here = slice(t * 256, t * 256 + 256)
        image[:, here] = image[:, here] + put[:32] + put[32:64] + put[64:]
    for p in range(2):
        for a, x in enumerate(split2(image[p * 16 : p * 16 + 16, :LOCAL])):
            zp[p, a * 48 + 32 : a * 48 + 48, :LOCAL] = x

    def inner(columns):
        made = jnp.zeros((48, 16), F32)
        for p in range(2):
            whole = zp[p, :, columns]
            for b in range(2):
                both = lax.dot_general(
                    whole, zp[p, b * 48 + 32 : b * 48 + 48, columns], NT,
                    preferred_element_type=F32,
                )
                made = made + both[:48] + both[48:]
        return made

    pack[...] = jnp.zeros((48, 128), F32)
    pack[:, :16] = inner(slice(0, LOCAL))
    wait_bytes(arrived.at[pl.ds(0, COLS - 1)], part_recv)
    bem_image = taken
    for k in range(COLS):
        bem_image = bem_image + arrived[k]
    image[:, LOCAL:] = bem_image
    for p in range(2):
        for a, x in enumerate(split2(bem_image[p * 16 : p * 16 + 16, :])):
            zp[p, a * 48 + 32 : a * 48 + 48, LOCAL:] = x
    pack[:, :16] = pack[:, :16] + inner(slice(LOCAL, WIDE))
    packed = pack[0:8, :]
    for g in range(1, 6):
        packed = packed + pltpu.roll(pack[8 * g : 8 * g + 8, :], 16 * g, 1)
    sum_out[:8, :] = packed
    reduce_cols()
    leave = pltpu.make_async_copy(image, w_hbm, out_sem)
    leave.start()

    for d, (exists, _, _, _) in enumerate(neighbours):

        @pl.when(exists)
        def _(d=d):
            wait_bytes(halo_out.at[d], halo_send.at[d])

    wait_bytes(phi.at[:, pl.ds(0, (ROWS - 1) * PIECE)], phi_send)
    wait_bytes(arrived.at[pl.ds(0, COLS - 1)], part_send)
    wait_bytes(swap_mid.at[pl.ds(0, ROWS - 1)], mid_send)
    wait_bytes(swap_in.at[:, pl.ds(0, COLS - 1), :], swap_send)
    reduce_rows()
    wait_bytes(col_in.at[pl.ds(0, COLS - 1)], col_send)
    leave.wait()
    sums[...] = reduced()
    wait_bytes(row_in.at[pl.ds(0, ROWS - 1)], row_send)


def finish_kernel(
    fem_hbm, bem_hbm, w_hbm, sums, next_fem, next_bem, hess, rfac,
    basis, image, pack_q, pack, fem_out, bem_out, in_sem, out_sem,
):
    copies = []
    for b in range(2):
        for p in range(2):
            rows = pl.ds(b * 16, 16)
            copies.append((fem_hbm.at[b, :, p, :], basis.at[p, rows, pl.ds(0, LOCAL)]))
            copies.append((bem_hbm.at[b, :, p, :], basis.at[p, rows, pl.ds(LOCAL, PIECE)]))
    copies.append((w_hbm, image))
    copies = [pltpu.make_async_copy(a, b, in_sem.at[i]) for i, (a, b) in enumerate(copies)]
    for copy in copies:
        copy.start()

    total = sums[8:, :]
    for g in range(4):
        pack_q[8 * g : 8 * g + 8, :] = total if g == 0 else pltpu.roll(total, 128 - 32 * g, 1)
    gram_q = pack_q[:, :32]
    total = sums[:8, :]
    for g in range(6):
        pack[8 * g : 8 * g + 8, :] = total if g == 0 else pltpu.roll(total, 128 - 16 * g, 1)
    one = pack[:32, :16]
    norm = pack[32:48, :16]

    both = 2.0 * one - small_dot(gram_q, one, ((1,), (0,)))
    hess[...] = both
    left = small_dot(gram_q, both, ((1,), (0,))) - one
    gram = norm + small_dot(both, left, ((0,), (0,))) - small_dot(one, both, ((0,), (0,)))
    row_id = lax.broadcasted_iota(jnp.int32, (16, 16), 0)
    col_id = lax.broadcasted_iota(jnp.int32, (16, 16), 1)
    work = (gram + gram.T) * 0.5
    inverse = (row_id == col_id).astype(F32)
    upper = jnp.zeros((16, 16), F32)
    lower_inv = jnp.zeros((16, 16), F32)
    for j in range(16):
        pivot = work[j : j + 1, j : j + 1]
        root = lax.rsqrt(pivot)
        root = root * (1.5 - 0.5 * pivot * root * root)
        line = jnp.broadcast_to(work[j : j + 1, :] * root, (16, 16))
        line_inv = jnp.broadcast_to(inverse[j : j + 1, :] * root, (16, 16))
        column = jnp.broadcast_to(work[:, j : j + 1] * root, (16, 16))
        upper = jnp.where((row_id == j) & (col_id >= j), line, upper)
        lower_inv = jnp.where(row_id == j, line_inv, lower_inv)
        work = work - column * line
        inverse = inverse - column * line_inv
    rfac[...] = upper

    weights = -small_dot(lower_inv, both, ((1,), (1,)))
    w_pair = jnp.concatenate(split2(weights), axis=0)
    l_pair = jnp.concatenate(split2(lower_inv), axis=0)
    for copy in copies:
        copy.wait()
    leaving = []
    for p in range(2):
        q_high, q_low = split2(basis[p])
        i_high, i_low = split2(image[p * 16 : p * 16 + 16, :])
        first = jnp.dot(w_pair, q_high, preferred_element_type=F32)
        first = first + jnp.dot(l_pair, i_high, preferred_element_type=F32)
        second = jnp.dot(w_pair[:16], q_low, preferred_element_type=F32)
        second = second + jnp.dot(l_pair[:16], i_low, preferred_element_type=F32)
        made = first[:16] + first[16:] + second
        fem_out[p] = made[:, :LOCAL]
        bem_out[p] = made[:, LOCAL:]
        leaving.append(pltpu.make_async_copy(fem_out.at[p], next_fem.at[:, p, :], out_sem.at[p]))
        leaving.append(
            pltpu.make_async_copy(bem_out.at[p], next_bem.at[:, p, :], out_sem.at[2 + p])
        )
        leaving[-2].start()
        leaving[-1].start()
    for copy in leaving:
        copy.wait()


def body(fem_basis, bem_basis, diag, vals, cols, halo, mat, trace, slot):
    vmem = pl.BlockSpec(memory_space=pltpu.VMEM)
    hbm = pl.BlockSpec(memory_space=pl.ANY)
    dma = pltpu.SemaphoreType.DMA
    image, sums = pl.pallas_call(
        step_kernel,
        out_shape=(
            jax.ShapeDtypeStruct((VEC, WIDE), F32),
            jax.ShapeDtypeStruct((16, 128), F32),
        ),
        in_specs=[hbm] * 9,
        out_specs=(hbm, vmem),
        scratch_shapes=[
            pltpu.VMEM((2, VEC, LOCAL), F32),
            pltpu.VMEM((2, VEC, PIECE), F32),
            pltpu.VMEM((1, LOCAL), F32),
            pltpu.VMEM((16, LOCAL), F32),
            pltpu.VMEM((16, LOCAL), jnp.int32),
            pltpu.VMEM((4, 128), jnp.int32),
            pltpu.VMEM((1, 256), jnp.int32),
            pltpu.VMEM((1, PIECE), jnp.int32),
            dma((20,)),
            dma,
            pltpu.VMEM((640, 256), BF16),
            pltpu.VMEM((16, 2560), jnp.int32),
            pltpu.VMEM((VEC, 1), F32),
            pltpu.VMEM((4, VEC, 128), F32),
            pltpu.VMEM((4, VEC, 128), F32),
            pltpu.VMEM((VEC, ROWS * PIECE), BF16),
            pltpu.VMEM((COLS, VEC, PIECE), F32),
            pltpu.VMEM((COLS, VEC, PIECE), F32),
            pltpu.VMEM((DEVICES, 128), F32),
            pltpu.VMEM((ROWS, COLS, 128), F32),
            pltpu.VMEM((ROWS, COLS, 128), F32),
            pltpu.VMEM((2, 2048, 1024), BF16),
            pltpu.VMEM((VEC, WIDE), F32),
            pltpu.VMEM((2, 96, WIDE), BF16),
            pltpu.VMEM((48, 128), F32),
            pltpu.VMEM((16, 128), F32),
            pltpu.VMEM((COLS, 16, 128), F32),
            pltpu.VMEM((ROWS, 16, 128), F32),
            dma((8,)),
            dma((4,)),
            dma((4,)),
            dma, dma, dma, dma, dma, dma, dma, dma,
            dma, dma, dma, dma,
        ],
        compiler_params=pltpu.CompilerParams(
            has_side_effects=True, collective_id=0, vmem_limit_bytes=60 << 20
        ),
    )(fem_basis, bem_basis, diag.reshape(1, LOCAL), vals, cols, halo, mat, trace.reshape(1, 256), slot.reshape(1, PIECE))
    next_fem, next_bem, hess, rfac = pl.pallas_call(
        finish_kernel,
        out_shape=(
            jax.ShapeDtypeStruct((16, 2, LOCAL), F32),
            jax.ShapeDtypeStruct((16, 2, PIECE), F32),
            jax.ShapeDtypeStruct((VEC, 16), F32),
            jax.ShapeDtypeStruct((16, 16), F32),
        ),
        in_specs=[hbm, hbm, hbm, vmem],
        out_specs=(hbm, hbm, vmem, vmem),
        scratch_shapes=[
            pltpu.VMEM((2, VEC, WIDE), F32),
            pltpu.VMEM((VEC, WIDE), F32),
            pltpu.VMEM((VEC, 128), F32),
            pltpu.VMEM((48, 128), F32),
            pltpu.VMEM((2, 16, LOCAL), F32),
            pltpu.VMEM((2, 16, PIECE), F32),
            dma((9,)),
            dma((4,)),
        ],
        compiler_params=pltpu.CompilerParams(vmem_limit_bytes=60 << 20),
    )(fem_basis, bem_basis, image, sums)
    return next_fem, next_bem, hess.reshape(2, 16, 16), rfac


def solution(mesh):
    both = ("row", "col")
    return jax.shard_map(
        body,
        mesh=mesh,
        in_specs=(
            P(None, None, None, both), P(None, None, None, both), P(both), P(None, both),
            P(None, both), P(None, both), P(None, "row", "col"), P(both), P(both),
        ),
        out_specs=(P(None, None, both), P(None, None, both), P(), P()),
        check_vma=False,
    )
```

```python
import functools

import jax
import jax.numpy as jnp
from jax import lax
from jax.experimental import pallas as pl
from jax.experimental.pallas import tpu as pltpu
from jax.sharding import PartitionSpec as P

F32 = jnp.float32
BF16 = jnp.bfloat16
MESH = pl.DeviceIdType.MESH
HIGHEST = lax.Precision.HIGHEST
ROWS, COLS = 8, 16
DEVICES = ROWS * COLS
VEC = 32
LOCAL = 2048
PIECE = 128
WIDE = LOCAL + PIECE
COUNT = 2.0 * DEVICES * (LOCAL + PIECE)
NT = (((1,), (1,)), ((), ()))
BY_LANE_NEAR = (1, 3, 5, 7, 9, 11, 13, 15)
BY_LANE_FAR = (1, 3, 5, 7, 9, 11, 13, 15)
BY_LANE_ALL = (1, 3, 5, 7, 9, 11, 13, 15)
FIRST_CHUNKS = 4
FAR_FIRST = (
    (2, 2), (2, 1), (2, 3), (1, 2), (3, 2), (2, 0), (0, 2), (1, 1), (1, 3), (3, 1), (3, 3),
    (1, 0), (3, 0), (0, 1), (0, 3),
)
ROW_STEPS = (4, 5, 3, 2, 6, 7, 1)


def split2(x):
    high = x.astype(BF16)
    return high, (x - high.astype(F32)).astype(BF16)


def split3(x):
    high = x.astype(BF16)
    rest = x - high.astype(F32)
    mid = rest.astype(BF16)
    return high, mid, (rest - mid.astype(F32)).astype(BF16)


def lane_gather(table, lanes):
    return jnp.take_along_axis(table, lanes, axis=1, mode="promise_in_bounds")


def small_dot(a, b, dims):
    return lax.dot_general(a, b, (dims, ((), ())), precision=HIGHEST, preferred_element_type=F32)


def paired(x):
    top = jnp.maximum(jnp.max(jnp.abs(x), axis=1, keepdims=True), 1e-30)
    whole = jnp.round(x * (32000.0 / top)).astype(jnp.int32)
    return (whole[:16] << 16) | (whole[16:] & 0xFFFF), top * (1.0 / 32000.0)


def looked_up(table, column, tiles, first):
    halves = []
    for half in range(2):
        here = jnp.broadcast_to(column[:, half * 128 : half * 128 + 128], (16, 128))
        low = here & 127
        high = here >> 7
        got = jnp.zeros((16, 128), jnp.int32)
        for t in range(tiles):
            got = jnp.where(high == t + first, lane_gather(table(t), low), got)
        halves.append(got)
    got = jnp.concatenate(halves, axis=1)
    return jnp.concatenate([got >> 16, (got << 16) >> 16], axis=0).astype(F32)


def multiplied_up(pieces, column, tiles, first):
    low = jnp.broadcast_to((column & 255).astype(jnp.int16), (256, 256))
    high = column >> 8
    hot = jnp.where(
        lax.broadcasted_iota(jnp.int16, (256, 256), 0) == low,
        jnp.ones((256, 256), BF16),
        jnp.zeros((256, 256), BF16),
    )
    found = jnp.dot(pieces, hot, preferred_element_type=F32)
    found = found[: tiles * VEC] + found[tiles * VEC :]
    got = jnp.zeros((VEC, 256), F32)
    for t in range(tiles):
        here = jnp.broadcast_to(high == t + first, (VEC, 256))
        got = jnp.where(here, found[t * VEC : t * VEC + VEC], got)
    return got


def step_kernel(
    fem_hbm, bem_hbm, diag_hbm, vals_hbm, cols_hbm, halo_hbm, mat, trace_hbm, slot_hbm,
    z_hbm, sums,
    fem, bem, diag, vals, cols, halo, trace, slot, in_sem, out_sem,
    near, pairs, unit, halo_out, halo_in, phi, partial, arrived, swap_out, swap_mid, swap_in,
    mat_buf, image, zp, pack, sum_out, col_in, row_in,
    mat_sem, halo_send, halo_recv, phi_send, phi_recv, part_send, part_recv,
    mid_send, mid_recv, swap_send, swap_recv, col_send, col_recv, row_send, row_recv,
):
    r = lax.axis_index("row")
    c = lax.axis_index("col")

    barrier = pltpu.get_barrier_semaphore()

    def greet_col(k, _):
        there = {"row": r, "col": lax.rem(c + k, COLS)}
        pl.semaphore_signal(barrier, inc=1, device_id=there, device_id_type=MESH)
        return 0

    def greet_row(k, _):
        there = {"row": lax.rem(r + k, ROWS), "col": c}
        pl.semaphore_signal(barrier, inc=1, device_id=there, device_id_type=MESH)
        return 0

    lax.fori_loop(1, ROWS, greet_row, 0)
    lax.fori_loop(1, COLS, greet_col, 0)

    loads = {}

    def load(name, pairs):
        first = 4 * len(loads)
        loads[name] = [
            pltpu.make_async_copy(a, b, in_sem.at[first + i]) for i, (a, b) in enumerate(pairs)
        ]
        for copy in loads[name]:
            copy.start()

    def ready(*names):
        for name in names:
            for copy in loads[name]:
                copy.wait()

    def parts(whole, held, blocks):
        return [
            (whole.at[b, :, p, :], held.at[b, pl.ds(p * 16, 16), :])
            for b in blocks
            for p in range(2)
        ]

    load("bem", parts(bem_hbm, bem, (0, 1)))
    load("fem", parts(fem_hbm, fem, (1,)))
    load("index", [(halo_hbm, halo), (trace_hbm, trace), (slot_hbm, slot)])
    load("sparse", [(cols_hbm, cols), (vals_hbm, vals), (diag_hbm, diag)])
    load("old", parts(fem_hbm, fem, (0,)))

    def chunk_at(k):
        y = lax.rem(c // 4 + 2 + 3 * (k // 2), 4)
        x = lax.rem(lax.rem(c, 4) // 2 + 1 + lax.rem(k, 2), 2)
        return 2 * y + x

    def matrix_copy(k):
        chunk = chunk_at(k)
        rows = pl.ds(pl.multiple_of(chunk * 256, 256), 256)
        return pltpu.make_async_copy(mat.at[:, rows, :], mat_buf.at[:, rows, :], mat_sem.at[k])

    for k in range(8):
        matrix_copy(k).start()

    def remote(src, dst, send, recv, row, col):
        return pltpu.make_async_remote_copy(
            src_ref=src, dst_ref=dst, send_sem=send, recv_sem=recv,
            device_id={"row": row, "col": col}, device_id_type=MESH,
        )

    def wait_bytes(ref, sem):
        pltpu.make_async_copy(ref, ref, sem).wait()

    ready("bem")
    mine = pl.ds(pl.multiple_of(r * PIECE, PIECE), PIECE)
    phi[:, mine] = bem[1].astype(BF16)

    ready("index", "fem")

    def picked(rows):
        rows = jnp.broadcast_to(rows, (VEC, 128))
        high = rows >> 7
        low = rows & 127
        out = jnp.zeros((VEC, 128), F32)
        for t in range(LOCAL // 128):
            out = jnp.where(high == t, lane_gather(fem[1, :, t * 128 : (t + 1) * 128], low), out)
        return out

    for d in range(4):
        halo_out[d] = picked(halo[d : d + 1, :])
    for d, missing in enumerate((c == 0, c == COLS - 1, r == 0, r == ROWS - 1)):

        @pl.when(missing)
        def _(d=d):
            halo_in[d] = jnp.zeros((VEC, 128), F32)

    pl.semaphore_wait(barrier, ROWS + COLS - 2)

    for k in ROW_STEPS:
        other = lax.rem(r + k, ROWS)
        remote(phi.at[:, mine], phi.at[:, mine], phi_send, phi_recv, other, c).start()

    neighbours = (
        (c + 1 < COLS, r, c + 1, c > 0),
        (c > 0, r, c - 1, c + 1 < COLS),
        (r + 1 < ROWS, r + 1, c, r > 0),
        (r > 0, r - 1, c, r + 1 < ROWS),
    )
    for d, (exists, row, col, _) in enumerate(neighbours):

        @pl.when(exists)
        def _(d=d, row=row, col=col):
            remote(
                halo_out.at[d], halo_in.at[d], halo_send.at[d], halo_recv.at[d], row, col
            ).start()

    lane = lax.broadcasted_iota(jnp.int32, (8, 128), 1)
    trace_lo = jnp.broadcast_to(trace[:, :128], (8, 128))
    trace_hi = jnp.broadcast_to(trace[:, 128:], (8, 128))
    trace_q = []
    for q in range(2):
        source = (2 * lane + q) & 127
        full = jnp.where(lane < 64, lane_gather(trace_lo, source), lane_gather(trace_hi, source))
        trace_q.append(full[:1])
    leaving = [picked(jnp.maximum(t, 0)) * (t >= 0).astype(F32) for t in trace_q]
    owner = lax.broadcasted_iota(jnp.int32, (2 * DEVICES, PIECE), 0)
    owner = jnp.where(owner < DEVICES, 2 * owner, 2 * (owner - DEVICES) + 1)
    places = (owner == slot[...]).astype(F32).astype(BF16)
    back = lax.dot_general(
        jnp.concatenate(split3(bem[1]), axis=0), places, NT, preferred_element_type=F32
    )
    back = back[:VEC] + back[VEC : 2 * VEC] + back[2 * VEC :]
    swap_out[...] = jnp.concatenate(leaving + [back[:, :128], back[:, 128:]], axis=0).T

    for k in ROW_STEPS:
        other = lax.rem(r + k, ROWS)
        block = pl.ds(pl.multiple_of(other * COLS, COLS), COLS)
        remote(swap_out.at[block], swap_mid.at[r], mid_send, mid_recv, other, c).start()
    swap_mid[r] = swap_out[pl.ds(pl.multiple_of(r * COLS, COLS), COLS)]

    def gathered(groups, width):
        made = jnp.zeros((8, 128), F32)
        for g in range(groups):
            x = pack[8 * g : 8 * g + 8, :]
            x = jnp.where(lane < width, x + pltpu.roll(x, 128 - width, 1), 0.0)
            made = made + (x if g == 0 else pltpu.roll(x, width * g, 1))
        return made

    ready("old")
    for p in range(2):
        rows = slice(p * 16, p * 16 + 16)
        for b in range(2):
            for a, x in enumerate(split2(fem[b, rows, :])):
                zp[p, a * 48 + b * 16 : a * 48 + b * 16 + 16, :LOCAL] = x
            for a, x in enumerate(split2(bem[b, rows, :])):
                zp[p, a * 48 + b * 16 : a * 48 + b * 16 + 16, LOCAL:] = x
    own = jnp.zeros((2 * VEC, 2 * VEC), F32)
    for p in range(2):
        whole = jnp.concatenate([zp[p, :32, :], zp[p, 48:80, :]], axis=0)
        own = own + lax.dot_general(whole, whole, NT, preferred_element_type=F32)
    pack[...] = jnp.zeros((48, 128), F32)
    pack[:32, :64] = own[:32] + own[32:]
    sum_out[8:, :] = gathered(4, 32)

    for t in range(8):
        for a, piece in enumerate(split2(fem[1, :, t * 256 : (t + 1) * 256])):
            near[a * 320 + t * 32 : a * 320 + t * 32 + 32, :] = piece
    pairs[:, :LOCAL], unit[...] = paired(fem[1])
    ready("sparse")

    def product(j, where, tiles, first, by_lane, start):
        here = pl.ds(pl.multiple_of(j * 256, 256), 256)
        acc = start(here)
        lane_acc = jnp.zeros((VEC, 256), F32)
        high = where[first * VEC : (first + tiles) * VEC, :]
        low = where[(10 + first) * VEC : (10 + first + tiles) * VEC, :]
        pieces = jnp.concatenate([high, low], axis=0)
        for k in range(16):
            column = cols[k : k + 1, here]
            value = vals[k : k + 1, here]
            if k in by_lane:
                got = looked_up(
                    lambda t: pairs[:, (2 * first + t) * 128 : (2 * first + t + 1) * 128],
                    column, 2 * tiles, 2 * first,
                )
                lane_acc = lane_acc + value * got
            else:
                acc = acc + value * multiplied_up(pieces, column, tiles, first)
        image[:, here] = acc + lane_acc * unit[...]
        return 0

    def diagonal(here):
        return diag[:, here] * fem[1, :, here]

    def product_near(j, _):
        return product(j, near, 8, 0, BY_LANE_NEAR, diagonal)

    def product_far(j, _):
        return product(j, near, 2, 8, BY_LANE_FAR, lambda here: image[:, here])

    def product_all(j, _):
        return product(j, near, 10, 0, BY_LANE_ALL, diagonal)

    lax.fori_loop(0, FIRST_CHUNKS, product_near, 0)

    wait_bytes(swap_mid.at[pl.ds(0, ROWS - 1)], mid_recv)

    for dy, dx in FAR_FIRST:
        other = lax.rem(c // 4 + dy, 4) * 4 + lax.rem(c + dx, 4)
        remote(
            swap_mid.at[:, pl.ds(other, 1), :], swap_in.at[:, pl.ds(c, 1), :],
            swap_send, swap_recv, r, other,
        ).start()
    swap_in[:, pl.ds(c, 1), :] = swap_mid[:, pl.ds(c, 1), :]

    wait_bytes(phi.at[:, pl.ds(0, (ROWS - 1) * PIECE)], phi_recv)
    phi_all = phi[...]
    turned = jnp.concatenate([-phi_all[16:], phi_all[:16]], axis=0)

    def multiply(k, _):
        chunk = chunk_at(k)
        matrix_copy(k).wait()
        rows = pl.ds(pl.multiple_of(chunk * 256, 256), 256)
        out = lax.dot_general(phi_all, mat_buf[0, rows, :], NT, preferred_element_type=F32)
        out = out + lax.dot_general(turned, mat_buf[1, rows, :], NT, preferred_element_type=F32)
        for half in range(2):
            other = 2 * chunk + half
            partial[other] = out[:, half * 128 : half * 128 + 128]

            @pl.when(other != c)
            def _():
                remote(partial.at[other], arrived.at[c], part_send, part_recv, r, other).start()

        return 0

    lax.fori_loop(0, 8, multiply, 0)
    arrived[c] = partial[c]

    def reduce_cols():
        col_in[c] = sum_out[...]

        for dy, dx in FAR_FIRST:
            other = lax.rem(c // 4 + dy, 4) * 4 + lax.rem(c + dx, 4)
            remote(sum_out, col_in.at[c], col_send, col_recv, r, other).start()

    def reduce_rows():
        wait_bytes(col_in.at[pl.ds(0, COLS - 1)], col_recv)
        total = col_in[0]
        for k in range(1, COLS):
            total = total + col_in[k]
        row_in[r] = total

        for k in ROW_STEPS:
            other = lax.rem(r + k, ROWS)
            remote(row_in.at[r], row_in.at[r], row_send, row_recv, other, c).start()

    def reduced():
        wait_bytes(row_in.at[pl.ds(0, ROWS - 1)], row_recv)
        total = row_in[0]
        for k in range(1, ROWS):
            total = total + row_in[k]
        return total * (1.0 / COUNT)

    for d, (_, _, _, comes) in enumerate(neighbours):

        @pl.when(comes)
        def _(d=d):
            wait_bytes(halo_in.at[d], halo_recv.at[d])

    outer = jnp.concatenate([halo_in[d] for d in range(4)], axis=1)
    for t in range(2):
        for a, piece in enumerate(split2(outer[:, t * 256 : t * 256 + 256])):
            near[a * 320 + 256 + t * 32 : a * 320 + 288 + t * 32, :] = piece
    pairs[...], unit[...] = paired(jnp.concatenate([fem[1], outer], axis=1))
    lax.fori_loop(0, FIRST_CHUNKS, product_far, 0)
    lax.fori_loop(FIRST_CHUNKS, LOCAL // 256, product_all, 0)

    wait_bytes(swap_in.at[:, pl.ds(0, COLS - 1), :], swap_recv)
    met = swap_in[...].reshape(DEVICES, 128).T
    chosen = jnp.broadcast_to(slot[...], (VEC, PIECE))
    taken = jnp.where(
        (chosen & 1) == 0, lane_gather(met[:32], chosen >> 1), lane_gather(met[32:64], chosen >> 1)
    )
    answers = jnp.concatenate([met[64:96], met[96:]], axis=1)
    answers = jnp.concatenate(split3(answers), axis=0)
    targets = jnp.concatenate(trace_q, axis=1).astype(jnp.int16)
    targets = jnp.broadcast_to(targets, (256, 256))
    for t in range(LOCAL // 256):
        row = lax.broadcasted_iota(jnp.int16, (256, 256), 0) + jnp.int16(t * 256)
        hot = jnp.where(row == targets, jnp.ones((256, 256), BF16), jnp.zeros((256, 256), BF16))
        put = lax.dot_general(answers, hot, NT, preferred_element_type=F32)
        here = slice(t * 256, t * 256 + 256)
        image[:, here] = image[:, here] + put[:32] + put[32:64] + put[64:]
    for p in range(2):
        for a, x in enumerate(split2(image[p * 16 : p * 16 + 16, :LOCAL])):
            zp[p, a * 48 + 32 : a * 48 + 48, :LOCAL] = x

    def inner(columns):
        made = jnp.zeros((96, 32), F32)
        for p in range(2):
            images = jnp.concatenate([zp[p, 32:48, columns], zp[p, 80:96, columns]], axis=0)
            made = made + lax.dot_general(
                zp[p, :, columns], images, NT, preferred_element_type=F32
            )
        return made[:48] + made[48:]

    pack[...] = jnp.zeros((48, 128), F32)
    pack[:, :32] = inner(slice(0, LOCAL))
    wait_bytes(arrived.at[pl.ds(0, COLS - 1)], part_recv)
    bem_image = taken
    for k in range(COLS):
        bem_image = bem_image + arrived[k]
    for p in range(2):
        for a, x in enumerate(split2(bem_image[p * 16 : p * 16 + 16, :])):
            zp[p, a * 48 + 32 : a * 48 + 48, LOCAL:] = x
    pack[:, :32] = pack[:, :32] + inner(slice(LOCAL, WIDE))
    sum_out[:8, :] = gathered(6, 16)
    reduce_cols()
    leave = pltpu.make_async_copy(zp, z_hbm, out_sem)
    leave.start()

    for d, (exists, _, _, _) in enumerate(neighbours):

        @pl.when(exists)
        def _(d=d):
            wait_bytes(halo_out.at[d], halo_send.at[d])

    wait_bytes(phi.at[:, pl.ds(0, (ROWS - 1) * PIECE)], phi_send)
    wait_bytes(arrived.at[pl.ds(0, COLS - 1)], part_send)
    wait_bytes(swap_mid.at[pl.ds(0, ROWS - 1)], mid_send)
    wait_bytes(swap_in.at[:, pl.ds(0, COLS - 1), :], swap_send)
    reduce_rows()
    wait_bytes(col_in.at[pl.ds(0, COLS - 1)], col_send)
    leave.wait()
    sums[...] = reduced()
    wait_bytes(row_in.at[pl.ds(0, ROWS - 1)], row_send)


def finish_kernel(
    z_hbm, sums, next_fem, next_bem, hess, rfac,
    zp, pack_q, pack, wide, fem_out, bem_out, in_sem, out_sem,
):
    copies = [pltpu.make_async_copy(z_hbm.at[p], zp.at[p], in_sem.at[p]) for p in range(2)]
    for copy in copies:
        copy.start()

    total = sums[8:, :]
    for g in range(4):
        pack_q[8 * g : 8 * g + 8, :] = total if g == 0 else pltpu.roll(total, 128 - 32 * g, 1)
    gram_q = pack_q[:, :32]
    total = sums[:8, :]
    for g in range(6):
        pack[8 * g : 8 * g + 8, :] = total if g == 0 else pltpu.roll(total, 128 - 16 * g, 1)
    one = pack[:32, :16]
    norm = pack[32:48, :16]

    both = 2.0 * one - small_dot(gram_q, one, ((1,), (0,)))
    hess[...] = both
    left = small_dot(gram_q, both, ((1,), (0,))) - one
    gram = norm + small_dot(both, left, ((0,), (0,))) - small_dot(one, both, ((0,), (0,)))
    row_id = lax.broadcasted_iota(jnp.int32, (16, 128), 0)
    col_id = lax.broadcasted_iota(jnp.int32, (16, 128), 1)
    wide[...] = (col_id == row_id + 16).astype(F32)
    wide[:, :16] = (gram + gram.T) * 0.5
    work = wide[...]
    rows = jnp.zeros((16, 128), F32)
    for j in range(0, 16, 2):
        line_a = jnp.broadcast_to(work[j : j + 1, :], (16, 128))
        line_b = jnp.broadcast_to(work[j + 1 : j + 2, :], (16, 128))
        col_a = jnp.broadcast_to(work[:, j : j + 1], (16, 128))
        col_b = jnp.broadcast_to(work[:, j + 1 : j + 2], (16, 128))
        aa = jnp.broadcast_to(col_a[j : j + 1, :], (16, 128))
        ab = jnp.broadcast_to(col_b[j : j + 1, :], (16, 128))
        bb = jnp.broadcast_to(col_b[j + 1 : j + 2, :], (16, 128))
        second = line_b - line_a * (ab / aa)
        rows = jnp.where(row_id == j, line_a, jnp.where(row_id == j + 1, second, rows))
        if j < 14:
            scale = 1.0 / (bb - ab * (ab / aa))
            step = (col_b - col_a * (ab / aa)) * scale
            work = work - col_a * (line_a / aa) - step * second
    pivot = jnp.sum(jnp.where(row_id == col_id, rows, 0.0), axis=1, keepdims=True)
    root = lax.rsqrt(pivot)
    root = root * (1.5 - 0.5 * pivot * root * root)
    rows = rows * root
    wide[...] = jnp.where(row_id <= col_id, rows, 0.0)
    rfac[...] = wide[:, :16]
    wide[...] = pltpu.roll(rows, 112, 1)
    lower_inv = wide[:, :16]

    weights = -small_dot(lower_inv, both, ((1,), (1,)))
    w_pair = jnp.concatenate(split2(weights), axis=0)
    l_pair = jnp.concatenate(split2(lower_inv), axis=0)
    leaving = []
    for p in range(2):
        copies[p].wait()
        first = jnp.dot(w_pair, zp[p, :32, :], preferred_element_type=F32)
        first = first + jnp.dot(l_pair, zp[p, 32:48, :], preferred_element_type=F32)
        second = jnp.dot(w_pair[:16], zp[p, 48:80, :], preferred_element_type=F32)
        second = second + jnp.dot(l_pair[:16], zp[p, 80:, :], preferred_element_type=F32)
        made = first[:16] + first[16:] + second
        fem_out[p] = made[:, :LOCAL]
        bem_out[p] = made[:, LOCAL:]
        leaving.append(pltpu.make_async_copy(fem_out.at[p], next_fem.at[:, p, :], out_sem.at[p]))
        leaving.append(
            pltpu.make_async_copy(bem_out.at[p], next_bem.at[:, p, :], out_sem.at[2 + p])
        )
        leaving[-2].start()
        leaving[-1].start()
    for copy in leaving:
        copy.wait()


def body(fem_basis, bem_basis, diag, vals, cols, halo, mat, trace, slot):
    vmem = pl.BlockSpec(memory_space=pltpu.VMEM)
    hbm = pl.BlockSpec(memory_space=pl.ANY)
    dma = pltpu.SemaphoreType.DMA
    halves, sums = pl.pallas_call(
        step_kernel,
        out_shape=(
            jax.ShapeDtypeStruct((2, 96, WIDE), BF16),
            jax.ShapeDtypeStruct((16, 128), F32),
        ),
        in_specs=[hbm] * 9,
        out_specs=(hbm, vmem),
        scratch_shapes=[
            pltpu.VMEM((2, VEC, LOCAL), F32),
            pltpu.VMEM((2, VEC, PIECE), F32),
            pltpu.VMEM((1, LOCAL), F32),
            pltpu.VMEM((16, LOCAL), F32),
            pltpu.VMEM((16, LOCAL), jnp.int32),
            pltpu.VMEM((4, 128), jnp.int32),
            pltpu.VMEM((1, 256), jnp.int32),
            pltpu.VMEM((1, PIECE), jnp.int32),
            dma((20,)),
            dma,
            pltpu.VMEM((640, 256), BF16),
            pltpu.VMEM((16, 2560), jnp.int32),
            pltpu.VMEM((VEC, 1), F32),
            pltpu.VMEM((4, VEC, 128), F32),
            pltpu.VMEM((4, VEC, 128), F32),
            pltpu.VMEM((VEC, ROWS * PIECE), BF16),
            pltpu.VMEM((COLS, VEC, PIECE), F32),
            pltpu.VMEM((COLS, VEC, PIECE), F32),
            pltpu.VMEM((DEVICES, 128), F32),
            pltpu.VMEM((ROWS, COLS, 128), F32),
            pltpu.VMEM((ROWS, COLS, 128), F32),
            pltpu.VMEM((2, 2048, 1024), BF16),
            pltpu.VMEM((VEC, LOCAL), F32),
            pltpu.VMEM((2, 96, WIDE), BF16),
            pltpu.VMEM((48, 128), F32),
            pltpu.VMEM((16, 128), F32),
            pltpu.VMEM((COLS, 16, 128), F32),
            pltpu.VMEM((ROWS, 16, 128), F32),
            dma((8,)),
            dma((4,)),
            dma((4,)),
            dma, dma, dma, dma, dma, dma, dma, dma,
            dma, dma, dma, dma,
        ],
        compiler_params=pltpu.CompilerParams(
            has_side_effects=True, collective_id=0, vmem_limit_bytes=60 << 20
        ),
    )(fem_basis, bem_basis, diag.reshape(1, LOCAL), vals, cols, halo, mat, trace.reshape(1, 256), slot.reshape(1, PIECE))
    next_fem, next_bem, hess, rfac = pl.pallas_call(
        finish_kernel,
        out_shape=(
            jax.ShapeDtypeStruct((16, 2, LOCAL), F32),
            jax.ShapeDtypeStruct((16, 2, PIECE), F32),
            jax.ShapeDtypeStruct((VEC, 16), F32),
            jax.ShapeDtypeStruct((16, 16), F32),
        ),
        in_specs=[hbm, vmem],
        out_specs=(hbm, hbm, vmem, vmem),
        scratch_shapes=[
            pltpu.VMEM((2, 96, WIDE), BF16),
            pltpu.VMEM((VEC, 128), F32),
            pltpu.VMEM((48, 128), F32),
            pltpu.VMEM((16, 128), F32),
            pltpu.VMEM((2, 16, LOCAL), F32),
            pltpu.VMEM((2, 16, PIECE), F32),
            dma((2,)),
            dma((4,)),
        ],
        compiler_params=pltpu.CompilerParams(vmem_limit_bytes=60 << 20),
    )(halves, sums)
    return next_fem, next_bem, hess.reshape(2, 16, 16), rfac


def solution(mesh):
    both = ("row", "col")
    return jax.shard_map(
        body,
        mesh=mesh,
        in_specs=(
            P(None, None, None, both), P(None, None, None, both), P(both), P(None, both),
            P(None, both), P(None, both), P(None, "row", "col"), P(both), P(both),
        ),
        out_specs=(P(None, None, both), P(None, None, both), P(), P()),
        check_vma=False,
    )
```

```python
import functools

import jax
import jax.numpy as jnp
from jax import lax
from jax.experimental import pallas as pl
from jax.experimental.pallas import tpu as pltpu
from jax.sharding import PartitionSpec as P

F32 = jnp.float32
BF16 = jnp.bfloat16
MESH = pl.DeviceIdType.MESH
HIGHEST = lax.Precision.HIGHEST
ROWS, COLS = 8, 16
DEVICES = ROWS * COLS
VEC = 32
LOCAL = 2048
PIECE = 128
WIDE = LOCAL + PIECE
COUNT = 2.0 * DEVICES * (LOCAL + PIECE)
NT = (((1,), (1,)), ((), ()))
BY_LANE_NEAR = (1, 3, 5, 7, 9, 11, 13, 15)
BY_LANE_FAR = (1, 3, 5, 7, 9, 11, 13, 15)
BY_LANE_ALL = (1, 3, 5, 7, 9, 11, 13, 15)
FIRST_CHUNKS = 5
FAR_FIRST = (
    (2, 2), (2, 1), (2, 3), (1, 2), (3, 2), (2, 0), (0, 2), (1, 1), (1, 3), (3, 1), (3, 3),
    (1, 0), (3, 0), (0, 1), (0, 3),
)
ROW_STEPS = (4, 5, 3, 2, 6, 7, 1)


def split2(x):
    high = x.astype(BF16)
    return high, (x - high.astype(F32)).astype(BF16)


def split3(x):
    high = x.astype(BF16)
    rest = x - high.astype(F32)
    mid = rest.astype(BF16)
    return high, mid, (rest - mid.astype(F32)).astype(BF16)


def lane_gather(table, lanes):
    return jnp.take_along_axis(table, lanes, axis=1, mode="promise_in_bounds")


def small_dot(a, b, dims):
    return lax.dot_general(a, b, (dims, ((), ())), precision=HIGHEST, preferred_element_type=F32)


def paired(x):
    top = jnp.maximum(jnp.max(jnp.abs(x), axis=1, keepdims=True), 1e-30)
    whole = jnp.round(x * (32000.0 / top)).astype(jnp.int32)
    return (whole[:16] << 16) | (whole[16:] & 0xFFFF), top * (1.0 / 32000.0)


def looked_up(table, column, tiles, first):
    halves = []
    for half in range(2):
        here = jnp.broadcast_to(column[:, half * 128 : half * 128 + 128], (16, 128))
        low = here & 127
        high = here >> 7
        got = jnp.zeros((16, 128), jnp.int32)
        for t in range(tiles):
            got = jnp.where(high == t + first, lane_gather(table(t), low), got)
        halves.append(got)
    got = jnp.concatenate(halves, axis=1)
    return jnp.concatenate([got >> 16, (got << 16) >> 16], axis=0).astype(F32)


def multiplied_up(pieces, column, tiles, first):
    low = jnp.broadcast_to((column & 255).astype(jnp.int16), (256, 256))
    high = column >> 8
    hot = jnp.where(
        lax.broadcasted_iota(jnp.int16, (256, 256), 0) == low,
        jnp.ones((256, 256), BF16),
        jnp.zeros((256, 256), BF16),
    )
    found = jnp.dot(pieces, hot, preferred_element_type=F32)
    found = found[: tiles * VEC] + found[tiles * VEC :]
    got = jnp.zeros((VEC, 256), F32)
    for t in range(tiles):
        here = jnp.broadcast_to(high == t + first, (VEC, 256))
        got = jnp.where(here, found[t * VEC : t * VEC + VEC], got)
    return got


def step_kernel(
    fem_hbm, bem_hbm, diag_hbm, vals_hbm, cols_hbm, halo_hbm, mat, trace_hbm, slot_hbm,
    z_hbm, sums,
    fem, bem, diag, vals, cols, halo, trace, slot, in_sem, out_sem,
    near, pairs, unit, halo_out, halo_in, phi, partial, arrived, swap_out, swap_mid, swap_in,
    mat_buf, image, zp, pack, sum_out, col_in, row_in,
    mat_sem, halo_send, halo_recv, phi_send, phi_recv, part_send, part_recv,
    mid_send, mid_recv, swap_send, swap_recv, col_send, col_recv, row_send, row_recv,
):
    r = lax.axis_index("row")
    c = lax.axis_index("col")

    barrier = pltpu.get_barrier_semaphore()

    def greet_col(k, _):
        there = {"row": r, "col": lax.rem(c + k, COLS)}
        pl.semaphore_signal(barrier, inc=1, device_id=there, device_id_type=MESH)
        return 0

    def greet_row(k, _):
        there = {"row": lax.rem(r + k, ROWS), "col": c}
        pl.semaphore_signal(barrier, inc=1, device_id=there, device_id_type=MESH)
        return 0

    lax.fori_loop(1, ROWS, greet_row, 0)
    lax.fori_loop(1, COLS, greet_col, 0)

    loads = {}

    def load(name, pairs):
        first = 4 * len(loads)
        loads[name] = [
            pltpu.make_async_copy(a, b, in_sem.at[first + i]) for i, (a, b) in enumerate(pairs)
        ]
        for copy in loads[name]:
            copy.start()

    def ready(*names):
        for name in names:
            for copy in loads[name]:
                copy.wait()

    def parts(whole, held, blocks):
        return [
            (whole.at[b, :, p, :], held.at[b, pl.ds(p * 16, 16), :])
            for b in blocks
            for p in range(2)
        ]

    load("bem", parts(bem_hbm, bem, (0, 1)))
    load("fem", parts(fem_hbm, fem, (1,)))
    load("index", [(halo_hbm, halo), (trace_hbm, trace), (slot_hbm, slot)])
    load("sparse", [(cols_hbm, cols), (vals_hbm, vals), (diag_hbm, diag)])
    load("old", parts(fem_hbm, fem, (0,)))

    def chunk_at(k):
        y = lax.rem(c // 4 + 2 + 3 * (k // 2), 4)
        x = lax.rem(lax.rem(c, 4) // 2 + 1 + lax.rem(k, 2), 2)
        return 2 * y + x

    def matrix_copy(k):
        chunk = chunk_at(k)
        rows = pl.ds(pl.multiple_of(chunk * 256, 256), 256)
        return pltpu.make_async_copy(mat.at[:, rows, :], mat_buf.at[:, rows, :], mat_sem.at[k])

    for k in range(8):
        matrix_copy(k).start()

    def remote(src, dst, send, recv, row, col):
        return pltpu.make_async_remote_copy(
            src_ref=src, dst_ref=dst, send_sem=send, recv_sem=recv,
            device_id={"row": row, "col": col}, device_id_type=MESH,
        )

    def wait_bytes(ref, sem):
        pltpu.make_async_copy(ref, ref, sem).wait()

    ready("bem")
    mine = pl.ds(pl.multiple_of(r * PIECE, PIECE), PIECE)
    phi[:, mine] = bem[1].astype(BF16)

    ready("index", "fem")

    def picked(rows):
        rows = jnp.broadcast_to(rows, (VEC, 128))
        high = rows >> 7
        low = rows & 127
        out = jnp.zeros((VEC, 128), F32)
        for t in range(LOCAL // 128):
            out = jnp.where(high == t, lane_gather(fem[1, :, t * 128 : (t + 1) * 128], low), out)
        return out

    for d in range(4):
        halo_out[d] = picked(halo[d : d + 1, :])
    for d, missing in enumerate((c == 0, c == COLS - 1, r == 0, r == ROWS - 1)):

        @pl.when(missing)
        def _(d=d):
            halo_in[d] = jnp.zeros((VEC, 128), F32)

    lane = lax.broadcasted_iota(jnp.int32, (8, 128), 1)
    trace_lo = jnp.broadcast_to(trace[:, :128], (8, 128))
    trace_hi = jnp.broadcast_to(trace[:, 128:], (8, 128))
    trace_q = []
    for q in range(2):
        source = (2 * lane + q) & 127
        full = jnp.where(lane < 64, lane_gather(trace_lo, source), lane_gather(trace_hi, source))
        trace_q.append(full[:1])
    leaving = [picked(jnp.maximum(t, 0)) * (t >= 0).astype(F32) for t in trace_q]
    owner = lax.broadcasted_iota(jnp.int32, (2 * DEVICES, PIECE), 0)
    owner = jnp.where(owner < DEVICES, 2 * owner, 2 * (owner - DEVICES) + 1)
    places = (owner == slot[...]).astype(F32).astype(BF16)
    back = lax.dot_general(
        jnp.concatenate(split3(bem[1]), axis=0), places, NT, preferred_element_type=F32
    )
    back = back[:VEC] + back[VEC : 2 * VEC] + back[2 * VEC :]
    swap_out[...] = jnp.concatenate(leaving + [back[:, :128], back[:, 128:]], axis=0).T

    pl.semaphore_wait(barrier, ROWS + COLS - 2)

    for k in ROW_STEPS:
        other = lax.rem(r + k, ROWS)
        remote(phi.at[:, mine], phi.at[:, mine], phi_send, phi_recv, other, c).start()

    neighbours = (
        (c + 1 < COLS, r, c + 1, c > 0),
        (c > 0, r, c - 1, c + 1 < COLS),
        (r + 1 < ROWS, r + 1, c, r > 0),
        (r > 0, r - 1, c, r + 1 < ROWS),
    )
    for d, (exists, row, col, _) in enumerate(neighbours):

        @pl.when(exists)
        def _(d=d, row=row, col=col):
            remote(
                halo_out.at[d], halo_in.at[d], halo_send.at[d], halo_recv.at[d], row, col
            ).start()

    for k in ROW_STEPS:
        other = lax.rem(r + k, ROWS)
        block = pl.ds(pl.multiple_of(other * COLS, COLS), COLS)
        remote(swap_out.at[block], swap_mid.at[r], mid_send, mid_recv, other, c).start()
    swap_mid[r] = swap_out[pl.ds(pl.multiple_of(r * COLS, COLS), COLS)]

    def gathered(groups, width):
        made = jnp.zeros((8, 128), F32)
        for g in range(groups):
            x = pack[8 * g : 8 * g + 8, :]
            x = jnp.where(lane < width, x + pltpu.roll(x, 128 - width, 1), 0.0)
            made = made + (x if g == 0 else pltpu.roll(x, width * g, 1))
        return made

    ready("old")
    for p in range(2):
        rows = slice(p * 16, p * 16 + 16)
        for b in range(2):
            for a, x in enumerate(split2(fem[b, rows, :])):
                zp[p, a * 48 + b * 16 : a * 48 + b * 16 + 16, :LOCAL] = x
            for a, x in enumerate(split2(bem[b, rows, :])):
                zp[p, a * 48 + b * 16 : a * 48 + b * 16 + 16, LOCAL:] = x
    own = jnp.zeros((2 * VEC, 2 * VEC), F32)
    for p in range(2):
        whole = jnp.concatenate([zp[p, :32, :], zp[p, 48:80, :]], axis=0)
        own = own + lax.dot_general(whole, whole, NT, preferred_element_type=F32)
    pack[...] = jnp.zeros((48, 128), F32)
    pack[:32, :64] = own[:32] + own[32:]
    sum_out[8:, :] = gathered(4, 32)

    for t in range(8):
        for a, piece in enumerate(split2(fem[1, :, t * 256 : (t + 1) * 256])):
            near[a * 320 + t * 32 : a * 320 + t * 32 + 32, :] = piece
    pairs[:, :LOCAL], unit[...] = paired(fem[1])
    ready("sparse")

    def product(j, where, tiles, first, by_lane, start):
        here = pl.ds(pl.multiple_of(j * 256, 256), 256)
        acc = start(here)
        lane_acc = jnp.zeros((VEC, 256), F32)
        high = where[first * VEC : (first + tiles) * VEC, :]
        low = where[(10 + first) * VEC : (10 + first + tiles) * VEC, :]
        pieces = jnp.concatenate([high, low], axis=0)
        for k in range(16):
            column = cols[k : k + 1, here]
            value = vals[k : k + 1, here]
            if k in by_lane:
                got = looked_up(
                    lambda t: pairs[:, (2 * first + t) * 128 : (2 * first + t + 1) * 128],
                    column, 2 * tiles, 2 * first,
                )
                lane_acc = lane_acc + value * got
            else:
                acc = acc + value * multiplied_up(pieces, column, tiles, first)
        image[:, here] = acc + lane_acc * unit[...]
        return 0

    def diagonal(here):
        return diag[:, here] * fem[1, :, here]

    def product_near(j, _):
        return product(j, near, 8, 0, BY_LANE_NEAR, diagonal)

    def product_far(j, _):
        return product(j, near, 2, 8, BY_LANE_FAR, lambda here: image[:, here])

    def product_all(j, _):
        return product(j, near, 10, 0, BY_LANE_ALL, diagonal)

    lax.fori_loop(0, FIRST_CHUNKS, product_near, 0)

    wait_bytes(swap_mid.at[pl.ds(0, ROWS - 1)], mid_recv)

    for dy, dx in FAR_FIRST:
        other = lax.rem(c // 4 + dy, 4) * 4 + lax.rem(c + dx, 4)
        remote(
            swap_mid.at[:, pl.ds(other, 1), :], swap_in.at[:, pl.ds(c, 1), :],
            swap_send, swap_recv, r, other,
        ).start()
    swap_in[:, pl.ds(c, 1), :] = swap_mid[:, pl.ds(c, 1), :]

    wait_bytes(phi.at[:, pl.ds(0, (ROWS - 1) * PIECE)], phi_recv)
    phi_all = phi[...]
    turned = jnp.concatenate([-phi_all[16:], phi_all[:16]], axis=0)

    def multiply(k, _):
        chunk = chunk_at(k)
        matrix_copy(k).wait()
        rows = pl.ds(pl.multiple_of(chunk * 256, 256), 256)
        out = lax.dot_general(phi_all, mat_buf[0, rows, :], NT, preferred_element_type=F32)
        out = out + lax.dot_general(turned, mat_buf[1, rows, :], NT, preferred_element_type=F32)
        for half in range(2):
            other = 2 * chunk + half
            partial[other] = out[:, half * 128 : half * 128 + 128]

            @pl.when(other != c)
            def _():
                remote(partial.at[other], arrived.at[c], part_send, part_recv, r, other).start()

        return 0

    lax.fori_loop(0, 8, multiply, 0)
    arrived[c] = partial[c]

    def reduce_cols():
        col_in[c] = sum_out[...]

        for dy, dx in FAR_FIRST:
            other = lax.rem(c // 4 + dy, 4) * 4 + lax.rem(c + dx, 4)
            remote(sum_out, col_in.at[c], col_send, col_recv, r, other).start()

    def reduce_rows():
        wait_bytes(col_in.at[pl.ds(0, COLS - 1)], col_recv)
        total = col_in[0]
        for k in range(1, COLS):
            total = total + col_in[k]
        row_in[r] = total

        for k in ROW_STEPS:
            other = lax.rem(r + k, ROWS)
            remote(row_in.at[r], row_in.at[r], row_send, row_recv, other, c).start()

    def reduced():
        wait_bytes(row_in.at[pl.ds(0, ROWS - 1)], row_recv)
        total = row_in[0]
        for k in range(1, ROWS):
            total = total + row_in[k]
        return total * (1.0 / COUNT)

    for d, (_, _, _, comes) in enumerate(neighbours):

        @pl.when(comes)
        def _(d=d):
            wait_bytes(halo_in.at[d], halo_recv.at[d])

    outer = jnp.concatenate([halo_in[d] for d in range(4)], axis=1)
    for t in range(2):
        for a, piece in enumerate(split2(outer[:, t * 256 : t * 256 + 256])):
            near[a * 320 + 256 + t * 32 : a * 320 + 288 + t * 32, :] = piece
    pairs[...], unit[...] = paired(jnp.concatenate([fem[1], outer], axis=1))
    lax.fori_loop(0, FIRST_CHUNKS, product_far, 0)
    lax.fori_loop(FIRST_CHUNKS, LOCAL // 256, product_all, 0)

    wait_bytes(swap_in.at[:, pl.ds(0, COLS - 1), :], swap_recv)
    met = swap_in[...].reshape(DEVICES, 128).T
    chosen = jnp.broadcast_to(slot[...], (VEC, PIECE))
    taken = jnp.where(
        (chosen & 1) == 0, lane_gather(met[:32], chosen >> 1), lane_gather(met[32:64], chosen >> 1)
    )
    answers = jnp.concatenate([met[64:96], met[96:]], axis=1)
    answers = jnp.concatenate(split3(answers), axis=0)
    targets = jnp.concatenate(trace_q, axis=1).astype(jnp.int16)
    targets = jnp.broadcast_to(targets, (256, 256))
    for t in range(LOCAL // 256):
        row = lax.broadcasted_iota(jnp.int16, (256, 256), 0) + jnp.int16(t * 256)
        hot = jnp.where(row == targets, jnp.ones((256, 256), BF16), jnp.zeros((256, 256), BF16))
        put = lax.dot_general(answers, hot, NT, preferred_element_type=F32)
        here = slice(t * 256, t * 256 + 256)
        image[:, here] = image[:, here] + put[:32] + put[32:64] + put[64:]
    for p in range(2):
        for a, x in enumerate(split2(image[p * 16 : p * 16 + 16, :LOCAL])):
            zp[p, a * 48 + 32 : a * 48 + 48, :LOCAL] = x

    def inner(columns):
        made = jnp.zeros((96, 32), F32)
        for p in range(2):
            images = jnp.concatenate([zp[p, 32:48, columns], zp[p, 80:96, columns]], axis=0)
            made = made + lax.dot_general(
                zp[p, :, columns], images, NT, preferred_element_type=F32
            )
        return made[:48] + made[48:]

    pack[...] = jnp.zeros((48, 128), F32)
    pack[:, :32] = inner(slice(0, LOCAL))
    wait_bytes(arrived.at[pl.ds(0, COLS - 1)], part_recv)
    bem_image = taken
    for k in range(COLS):
        bem_image = bem_image + arrived[k]
    for p in range(2):
        for a, x in enumerate(split2(bem_image[p * 16 : p * 16 + 16, :])):
            zp[p, a * 48 + 32 : a * 48 + 48, LOCAL:] = x
    pack[:, :32] = pack[:, :32] + inner(slice(LOCAL, WIDE))
    sum_out[:8, :] = gathered(6, 16)
    reduce_cols()
    leave = pltpu.make_async_copy(zp, z_hbm, out_sem)
    leave.start()

    for d, (exists, _, _, _) in enumerate(neighbours):

        @pl.when(exists)
        def _(d=d):
            wait_bytes(halo_out.at[d], halo_send.at[d])

    wait_bytes(phi.at[:, pl.ds(0, (ROWS - 1) * PIECE)], phi_send)
    wait_bytes(arrived.at[pl.ds(0, COLS - 1)], part_send)
    wait_bytes(swap_mid.at[pl.ds(0, ROWS - 1)], mid_send)
    wait_bytes(swap_in.at[:, pl.ds(0, COLS - 1), :], swap_send)
    reduce_rows()
    wait_bytes(col_in.at[pl.ds(0, COLS - 1)], col_send)
    leave.wait()
    sums[...] = reduced()
    wait_bytes(row_in.at[pl.ds(0, ROWS - 1)], row_send)


def finish_kernel(
    z_hbm, sums, next_fem, next_bem, hess, rfac,
    zp, pack_q, pack, wide, fem_out, bem_out, in_sem, out_sem,
):
    copies = [pltpu.make_async_copy(z_hbm.at[p], zp.at[p], in_sem.at[p]) for p in range(2)]
    for copy in copies:
        copy.start()

    total = sums[8:, :]
    for g in range(4):
        pack_q[8 * g : 8 * g + 8, :] = total if g == 0 else pltpu.roll(total, 128 - 32 * g, 1)
    gram_q = pack_q[:, :32]
    total = sums[:8, :]
    for g in range(6):
        pack[8 * g : 8 * g + 8, :] = total if g == 0 else pltpu.roll(total, 128 - 16 * g, 1)
    one = pack[:32, :16]
    norm = pack[32:48, :16]

    both = 2.0 * one - small_dot(gram_q, one, ((1,), (0,)))
    hess[...] = both
    left = small_dot(gram_q, both, ((1,), (0,))) - one
    gram = norm + small_dot(both, left, ((0,), (0,))) - small_dot(one, both, ((0,), (0,)))
    row_id = lax.broadcasted_iota(jnp.int32, (16, 128), 0)
    col_id = lax.broadcasted_iota(jnp.int32, (16, 128), 1)
    wide[...] = (col_id == row_id + 16).astype(F32)
    wide[:, :16] = (gram + gram.T) * 0.5
    work = wide[...]
    rows = jnp.zeros((16, 128), F32)
    for j in range(0, 16, 2):
        line_a = jnp.broadcast_to(work[j : j + 1, :], (16, 128))
        line_b = jnp.broadcast_to(work[j + 1 : j + 2, :], (16, 128))
        col_a = jnp.broadcast_to(work[:, j : j + 1], (16, 128))
        col_b = jnp.broadcast_to(work[:, j + 1 : j + 2], (16, 128))
        aa = jnp.broadcast_to(col_a[j : j + 1, :], (16, 128))
        ab = jnp.broadcast_to(col_b[j : j + 1, :], (16, 128))
        bb = jnp.broadcast_to(col_b[j + 1 : j + 2, :], (16, 128))
        second = line_b - line_a * (ab / aa)
        rows = jnp.where(row_id == j, line_a, jnp.where(row_id == j + 1, second, rows))
        if j < 14:
            scale = 1.0 / (bb - ab * (ab / aa))
            step = (col_b - col_a * (ab / aa)) * scale
            work = work - col_a * (line_a / aa) - step * second
    pivot = jnp.sum(jnp.where(row_id == col_id, rows, 0.0), axis=1, keepdims=True)
    root = lax.rsqrt(pivot)
    root = root * (1.5 - 0.5 * pivot * root * root)
    rows = rows * root
    wide[...] = jnp.where(row_id <= col_id, rows, 0.0)
    rfac[...] = wide[:, :16]
    wide[...] = pltpu.roll(rows, 112, 1)
    lower_inv = wide[:, :16]

    weights = -small_dot(lower_inv, both, ((1,), (1,)))
    w_pair = jnp.concatenate(split2(weights), axis=0)
    l_pair = jnp.concatenate(split2(lower_inv), axis=0)
    leaving = []
    for p in range(2):
        copies[p].wait()
        first = jnp.dot(w_pair, zp[p, :32, :], preferred_element_type=F32)
        first = first + jnp.dot(l_pair, zp[p, 32:48, :], preferred_element_type=F32)
        second = jnp.dot(w_pair[:16], zp[p, 48:80, :], preferred_element_type=F32)
        second = second + jnp.dot(l_pair[:16], zp[p, 80:, :], preferred_element_type=F32)
        made = first[:16] + first[16:] + second
        fem_out[p] = made[:, :LOCAL]
        bem_out[p] = made[:, LOCAL:]
        leaving.append(pltpu.make_async_copy(fem_out.at[p], next_fem.at[:, p, :], out_sem.at[p]))
        leaving.append(
            pltpu.make_async_copy(bem_out.at[p], next_bem.at[:, p, :], out_sem.at[2 + p])
        )
        leaving[-2].start()
        leaving[-1].start()
    for copy in leaving:
        copy.wait()


def body(fem_basis, bem_basis, diag, vals, cols, halo, mat, trace, slot):
    vmem = pl.BlockSpec(memory_space=pltpu.VMEM)
    hbm = pl.BlockSpec(memory_space=pl.ANY)
    dma = pltpu.SemaphoreType.DMA
    halves, sums = pl.pallas_call(
        step_kernel,
        out_shape=(
            jax.ShapeDtypeStruct((2, 96, WIDE), BF16),
            jax.ShapeDtypeStruct((16, 128), F32),
        ),
        in_specs=[hbm] * 9,
        out_specs=(hbm, vmem),
        scratch_shapes=[
            pltpu.VMEM((2, VEC, LOCAL), F32),
            pltpu.VMEM((2, VEC, PIECE), F32),
            pltpu.VMEM((1, LOCAL), F32),
            pltpu.VMEM((16, LOCAL), F32),
            pltpu.VMEM((16, LOCAL), jnp.int32),
            pltpu.VMEM((4, 128), jnp.int32),
            pltpu.VMEM((1, 256), jnp.int32),
            pltpu.VMEM((1, PIECE), jnp.int32),
            dma((20,)),
            dma,
            pltpu.VMEM((640, 256), BF16),
            pltpu.VMEM((16, 2560), jnp.int32),
            pltpu.VMEM((VEC, 1), F32),
            pltpu.VMEM((4, VEC, 128), F32),
            pltpu.VMEM((4, VEC, 128), F32),
            pltpu.VMEM((VEC, ROWS * PIECE), BF16),
            pltpu.VMEM((COLS, VEC, PIECE), F32),
            pltpu.VMEM((COLS, VEC, PIECE), F32),
            pltpu.VMEM((DEVICES, 128), F32),
            pltpu.VMEM((ROWS, COLS, 128), F32),
            pltpu.VMEM((ROWS, COLS, 128), F32),
            pltpu.VMEM((2, 2048, 1024), BF16),
            pltpu.VMEM((VEC, LOCAL), F32),
            pltpu.VMEM((2, 96, WIDE), BF16),
            pltpu.VMEM((48, 128), F32),
            pltpu.VMEM((16, 128), F32),
            pltpu.VMEM((COLS, 16, 128), F32),
            pltpu.VMEM((ROWS, 16, 128), F32),
            dma((8,)),
            dma((4,)),
            dma((4,)),
            dma, dma, dma, dma, dma, dma, dma, dma,
            dma, dma, dma, dma,
        ],
        compiler_params=pltpu.CompilerParams(
            has_side_effects=True, collective_id=0, vmem_limit_bytes=60 << 20
        ),
    )(fem_basis, bem_basis, diag.reshape(1, LOCAL), vals, cols, halo, mat, trace.reshape(1, 256), slot.reshape(1, PIECE))
    next_fem, next_bem, hess, rfac = pl.pallas_call(
        finish_kernel,
        out_shape=(
            jax.ShapeDtypeStruct((16, 2, LOCAL), F32),
            jax.ShapeDtypeStruct((16, 2, PIECE), F32),
            jax.ShapeDtypeStruct((VEC, 16), F32),
            jax.ShapeDtypeStruct((16, 16), F32),
        ),
        in_specs=[hbm, vmem],
        out_specs=(hbm, hbm, vmem, vmem),
        scratch_shapes=[
            pltpu.VMEM((2, 96, WIDE), BF16),
            pltpu.VMEM((VEC, 128), F32),
            pltpu.VMEM((48, 128), F32),
            pltpu.VMEM((16, 128), F32),
            pltpu.VMEM((2, 16, LOCAL), F32),
            pltpu.VMEM((2, 16, PIECE), F32),
            dma((2,)),
            dma((4,)),
        ],
        compiler_params=pltpu.CompilerParams(vmem_limit_bytes=60 << 20),
    )(halves, sums)
    return next_fem, next_bem, hess.reshape(2, 16, 16), rfac


def solution(mesh):
    both = ("row", "col")
    return jax.shard_map(
        body,
        mesh=mesh,
        in_specs=(
            P(None, None, None, both), P(None, None, None, both), P(both), P(None, both),
            P(None, both), P(None, both), P(None, "row", "col"), P(both), P(both),
        ),
        out_specs=(P(None, None, both), P(None, None, both), P(), P()),
        check_vma=False,
    )
```

```python
import functools

import jax
import jax.numpy as jnp
from jax import lax
from jax.experimental import pallas as pl
from jax.experimental.pallas import tpu as pltpu
from jax.sharding import PartitionSpec as P

F32 = jnp.float32
BF16 = jnp.bfloat16
MESH = pl.DeviceIdType.MESH
HIGHEST = lax.Precision.HIGHEST
ROWS, COLS = 8, 16
DEVICES = ROWS * COLS
VEC = 32
LOCAL = 2048
PIECE = 128
WIDE = LOCAL + PIECE
COUNT = 2.0 * DEVICES * (LOCAL + PIECE)
NT = (((1,), (1,)), ((), ()))
BY_LANE_NEAR = (1, 3, 5, 7, 9, 11, 13, 15)
BY_LANE_FAR = (1, 3, 5, 7, 9, 11, 13, 15)
BY_LANE_ALL = (1, 3, 5, 7, 9, 11, 13, 15)
FIRST_CHUNKS = 5
FAR_FIRST = (
    (2, 2), (2, 1), (2, 3), (1, 2), (3, 2), (2, 0), (0, 2), (1, 1), (1, 3), (3, 1), (3, 3),
    (1, 0), (3, 0), (0, 1), (0, 3),
)
ROW_STEPS = (4, 5, 3, 2, 6, 7, 1)


def split2(x):
    high = x.astype(BF16)
    return high, (x - high.astype(F32)).astype(BF16)


def split3(x):
    high = x.astype(BF16)
    rest = x - high.astype(F32)
    mid = rest.astype(BF16)
    return high, mid, (rest - mid.astype(F32)).astype(BF16)


def lane_gather(table, lanes):
    return jnp.take_along_axis(table, lanes, axis=1, mode="promise_in_bounds")


def small_dot(a, b, dims):
    return lax.dot_general(a, b, (dims, ((), ())), precision=HIGHEST, preferred_element_type=F32)


def paired(x):
    top = jnp.maximum(jnp.max(jnp.abs(x), axis=1, keepdims=True), 1e-30)
    whole = jnp.round(x * (32000.0 / top)).astype(jnp.int32)
    return (whole[:16] << 16) | (whole[16:] & 0xFFFF), top * (1.0 / 32000.0)


def looked_up(table, column, tiles, first):
    halves = []
    for half in range(2):
        here = jnp.broadcast_to(column[:, half * 128 : half * 128 + 128], (16, 128))
        low = here & 127
        high = here >> 7
        got = jnp.zeros((16, 128), jnp.int32)
        for t in range(tiles):
            got = jnp.where(high == t + first, lane_gather(table(t), low), got)
        halves.append(got)
    got = jnp.concatenate(halves, axis=1)
    return jnp.concatenate([got >> 16, (got << 16) >> 16], axis=0).astype(F32)


def multiplied_up(pieces, column, tiles, first):
    low = jnp.broadcast_to((column & 255).astype(jnp.int16), (256, 256))
    high = column >> 8
    hot = jnp.where(
        lax.broadcasted_iota(jnp.int16, (256, 256), 0) == low,
        jnp.ones((256, 256), BF16),
        jnp.zeros((256, 256), BF16),
    )
    found = jnp.dot(pieces, hot, preferred_element_type=F32)
    found = found[: tiles * VEC] + found[tiles * VEC :]
    got = jnp.zeros((VEC, 256), F32)
    for t in range(tiles):
        here = jnp.broadcast_to(high == t + first, (VEC, 256))
        got = jnp.where(here, found[t * VEC : t * VEC + VEC], got)
    return got


def step_kernel(
    fem_hbm, bem_hbm, diag_hbm, vals_hbm, cols_hbm, halo_hbm, mat, trace_hbm, slot_hbm,
    z_hbm, sums,
    fem, bem, diag, vals, cols, halo, trace, slot, in_sem, out_sem,
    near, pairs, unit, halo_out, halo_in, phi, partial, arrived, swap_out, swap_mid, swap_in,
    mat_buf, image, zp, pack, sum_out, col_in, row_in,
    mat_sem, halo_send, halo_recv, phi_send, phi_recv, part_send, part_recv,
    mid_send, mid_recv, swap_send, swap_recv, col_send, col_recv, row_send, row_recv,
):
    r = lax.axis_index("row")
    c = lax.axis_index("col")

    barrier = pltpu.get_barrier_semaphore()

    def greet_col(k, _):
        there = {"row": r, "col": lax.rem(c + k, COLS)}
        pl.semaphore_signal(barrier, inc=1, device_id=there, device_id_type=MESH)
        return 0

    def greet_row(k, _):
        there = {"row": lax.rem(r + k, ROWS), "col": c}
        pl.semaphore_signal(barrier, inc=1, device_id=there, device_id_type=MESH)
        return 0

    lax.fori_loop(1, ROWS, greet_row, 0)
    lax.fori_loop(1, COLS, greet_col, 0)

    loads = {}

    def load(name, pairs):
        first = 4 * len(loads)
        loads[name] = [
            pltpu.make_async_copy(a, b, in_sem.at[first + i]) for i, (a, b) in enumerate(pairs)
        ]
        for copy in loads[name]:
            copy.start()

    def ready(*names):
        for name in names:
            for copy in loads[name]:
                copy.wait()

    def parts(whole, held, blocks):
        return [
            (whole.at[b, :, p, :], held.at[b, pl.ds(p * 16, 16), :])
            for b in blocks
            for p in range(2)
        ]

    load("bem", parts(bem_hbm, bem, (0, 1)))
    load("fem", parts(fem_hbm, fem, (1,)))
    load("index", [(halo_hbm, halo), (trace_hbm, trace), (slot_hbm, slot)])
    load("sparse", [(cols_hbm, cols), (vals_hbm, vals), (diag_hbm, diag)])
    load("old", parts(fem_hbm, fem, (0,)))

    def chunk_at(k):
        y = lax.rem(c // 4 + 2 + 3 * (k // 2), 4)
        x = lax.rem(lax.rem(c, 4) // 2 + 1 + lax.rem(k, 2), 2)
        return 2 * y + x

    def matrix_copy(k):
        chunk = chunk_at(k)
        rows = pl.ds(pl.multiple_of(chunk * 256, 256), 256)
        return pltpu.make_async_copy(mat.at[:, rows, :], mat_buf.at[:, rows, :], mat_sem.at[k])

    def remote(src, dst, send, recv, row, col):
        return pltpu.make_async_remote_copy(
            src_ref=src, dst_ref=dst, send_sem=send, recv_sem=recv,
            device_id={"row": row, "col": col}, device_id_type=MESH,
        )

    def wait_bytes(ref, sem):
        pltpu.make_async_copy(ref, ref, sem).wait()

    ready("bem")
    for k in range(8):
        matrix_copy(k).start()
    mine = pl.ds(pl.multiple_of(r * PIECE, PIECE), PIECE)
    phi[:, mine] = bem[1].astype(BF16)

    ready("index", "fem")

    def picked(rows):
        rows = jnp.broadcast_to(rows, (VEC, 128))
        high = rows >> 7
        low = rows & 127
        out = jnp.zeros((VEC, 128), F32)
        for t in range(LOCAL // 128):
            out = jnp.where(high == t, lane_gather(fem[1, :, t * 128 : (t + 1) * 128], low), out)
        return out

    for d in range(4):
        halo_out[d] = picked(halo[d : d + 1, :])
    for d, missing in enumerate((c == 0, c == COLS - 1, r == 0, r == ROWS - 1)):

        @pl.when(missing)
        def _(d=d):
            halo_in[d] = jnp.zeros((VEC, 128), F32)

    lane = lax.broadcasted_iota(jnp.int32, (8, 128), 1)
    trace_lo = jnp.broadcast_to(trace[:, :128], (8, 128))
    trace_hi = jnp.broadcast_to(trace[:, 128:], (8, 128))
    trace_q = []
    for q in range(2):
        source = (2 * lane + q) & 127
        full = jnp.where(lane < 64, lane_gather(trace_lo, source), lane_gather(trace_hi, source))
        trace_q.append(full[:1])
    leaving = [picked(jnp.maximum(t, 0)) * (t >= 0).astype(F32) for t in trace_q]
    owner = lax.broadcasted_iota(jnp.int32, (2 * DEVICES, PIECE), 0)
    owner = jnp.where(owner < DEVICES, 2 * owner, 2 * (owner - DEVICES) + 1)
    places = (owner == slot[...]).astype(F32).astype(BF16)
    back = lax.dot_general(
        jnp.concatenate(split3(bem[1]), axis=0), places, NT, preferred_element_type=F32
    )
    back = back[:VEC] + back[VEC : 2 * VEC] + back[2 * VEC :]
    swap_out[...] = jnp.concatenate(leaving + [back[:, :128], back[:, 128:]], axis=0).T

    pl.semaphore_wait(barrier, ROWS + COLS - 2)

    for k in ROW_STEPS:
        other = lax.rem(r + k, ROWS)
        remote(phi.at[:, mine], phi.at[:, mine], phi_send, phi_recv, other, c).start()

    neighbours = (
        (c + 1 < COLS, r, c + 1, c > 0),
        (c > 0, r, c - 1, c + 1 < COLS),
        (r + 1 < ROWS, r + 1, c, r > 0),
        (r > 0, r - 1, c, r + 1 < ROWS),
    )
    for d, (exists, row, col, _) in enumerate(neighbours):

        @pl.when(exists)
        def _(d=d, row=row, col=col):
            remote(
                halo_out.at[d], halo_in.at[d], halo_send.at[d], halo_recv.at[d], row, col
            ).start()

    for k in ROW_STEPS:
        other = lax.rem(r + k, ROWS)
        block = pl.ds(pl.multiple_of(other * COLS, COLS), COLS)
        remote(swap_out.at[block], swap_mid.at[r], mid_send, mid_recv, other, c).start()
    swap_mid[r] = swap_out[pl.ds(pl.multiple_of(r * COLS, COLS), COLS)]

    def gathered(groups, width):
        made = jnp.zeros((8, 128), F32)
        for g in range(groups):
            x = pack[8 * g : 8 * g + 8, :]
            x = jnp.where(lane < width, x + pltpu.roll(x, 128 - width, 1), 0.0)
            made = made + (x if g == 0 else pltpu.roll(x, width * g, 1))
        return made

    ready("old")
    for p in range(2):
        rows = slice(p * 16, p * 16 + 16)
        for b in range(2):
            for a, x in enumerate(split2(fem[b, rows, :])):
                zp[p, a * 48 + b * 16 : a * 48 + b * 16 + 16, :LOCAL] = x
            for a, x in enumerate(split2(bem[b, rows, :])):
                zp[p, a * 48 + b * 16 : a * 48 + b * 16 + 16, LOCAL:] = x
    own = jnp.zeros((2 * VEC, 2 * VEC), F32)
    for p in range(2):
        whole = jnp.concatenate([zp[p, :32, :], zp[p, 48:80, :]], axis=0)
        own = own + lax.dot_general(whole, whole, NT, preferred_element_type=F32)
    pack[...] = jnp.zeros((48, 128), F32)
    pack[:32, :64] = own[:32] + own[32:]
    sum_out[8:, :] = gathered(4, 32)

    for t in range(8):
        for a, piece in enumerate(split2(fem[1, :, t * 256 : (t + 1) * 256])):
            near[a * 320 + t * 32 : a * 320 + t * 32 + 32, :] = piece
    pairs[:, :LOCAL], unit[...] = paired(fem[1])
    ready("sparse")

    def product(j, where, tiles, first, by_lane, start):
        here = pl.ds(pl.multiple_of(j * 256, 256), 256)
        acc = start(here)
        lane_acc = jnp.zeros((VEC, 256), F32)
        high = where[first * VEC : (first + tiles) * VEC, :]
        low = where[(10 + first) * VEC : (10 + first + tiles) * VEC, :]
        pieces = jnp.concatenate([high, low], axis=0)
        for k in range(16):
            column = cols[k : k + 1, here]
            value = vals[k : k + 1, here]
            if k in by_lane:
                got = looked_up(
                    lambda t: pairs[:, (2 * first + t) * 128 : (2 * first + t + 1) * 128],
                    column, 2 * tiles, 2 * first,
                )
                lane_acc = lane_acc + value * got
            else:
                acc = acc + value * multiplied_up(pieces, column, tiles, first)
        image[:, here] = acc + lane_acc * unit[...]
        return 0

    def diagonal(here):
        return diag[:, here] * fem[1, :, here]

    def product_near(j, _):
        return product(j, near, 8, 0, BY_LANE_NEAR, diagonal)

    def product_far(j, _):
        return product(j, near, 2, 8, BY_LANE_FAR, lambda here: image[:, here])

    def product_all(j, _):
        return product(j, near, 10, 0, BY_LANE_ALL, diagonal)

    lax.fori_loop(0, FIRST_CHUNKS, product_near, 0)

    wait_bytes(swap_mid.at[pl.ds(0, ROWS - 1)], mid_recv)

    for dy, dx in FAR_FIRST:
        other = lax.rem(c // 4 + dy, 4) * 4 + lax.rem(c + dx, 4)
        remote(
            swap_mid.at[:, pl.ds(other, 1), :], swap_in.at[:, pl.ds(c, 1), :],
            swap_send, swap_recv, r, other,
        ).start()
    swap_in[:, pl.ds(c, 1), :] = swap_mid[:, pl.ds(c, 1), :]

    wait_bytes(phi.at[:, pl.ds(0, (ROWS - 1) * PIECE)], phi_recv)
    phi_all = phi[...]
    turned = jnp.concatenate([-phi_all[16:], phi_all[:16]], axis=0)

    def multiply(k, _):
        chunk = chunk_at(k)
        matrix_copy(k).wait()
        rows = pl.ds(pl.multiple_of(chunk * 256, 256), 256)
        out = lax.dot_general(phi_all, mat_buf[0, rows, :], NT, preferred_element_type=F32)
        out = out + lax.dot_general(turned, mat_buf[1, rows, :], NT, preferred_element_type=F32)
        for half in range(2):
            other = 2 * chunk + half
            partial[other] = out[:, half * 128 : half * 128 + 128]

            @pl.when(other != c)
            def _():
                remote(partial.at[other], arrived.at[c], part_send, part_recv, r, other).start()

        return 0

    lax.fori_loop(0, 8, multiply, 0)
    arrived[c] = partial[c]

    def reduce_cols():
        col_in[c] = sum_out[...]

        for dy, dx in FAR_FIRST:
            other = lax.rem(c // 4 + dy, 4) * 4 + lax.rem(c + dx, 4)
            remote(sum_out, col_in.at[c], col_send, col_recv, r, other).start()

    def reduce_rows():
        wait_bytes(col_in.at[pl.ds(0, COLS - 1)], col_recv)
        total = col_in[0]
        for k in range(1, COLS):
            total = total + col_in[k]
        row_in[r] = total

        for k in ROW_STEPS:
            other = lax.rem(r + k, ROWS)
            remote(row_in.at[r], row_in.at[r], row_send, row_recv, other, c).start()

    def reduced():
        wait_bytes(row_in.at[pl.ds(0, ROWS - 1)], row_recv)
        total = row_in[0]
        for k in range(1, ROWS):
            total = total + row_in[k]
        return total * (1.0 / COUNT)

    for d, (_, _, _, comes) in enumerate(neighbours):

        @pl.when(comes)
        def _(d=d):
            wait_bytes(halo_in.at[d], halo_recv.at[d])

    outer = jnp.concatenate([halo_in[d] for d in range(4)], axis=1)
    for t in range(2):
        for a, piece in enumerate(split2(outer[:, t * 256 : t * 256 + 256])):
            near[a * 320 + 256 + t * 32 : a * 320 + 288 + t * 32, :] = piece
    pairs[...], unit[...] = paired(jnp.concatenate([fem[1], outer], axis=1))
    lax.fori_loop(0, FIRST_CHUNKS, product_far, 0)
    lax.fori_loop(FIRST_CHUNKS, LOCAL // 256, product_all, 0)

    wait_bytes(swap_in.at[:, pl.ds(0, COLS - 1), :], swap_recv)
    met = swap_in[...].reshape(DEVICES, 128).T
    chosen = jnp.broadcast_to(slot[...], (VEC, PIECE))
    taken = jnp.where(
        (chosen & 1) == 0, lane_gather(met[:32], chosen >> 1), lane_gather(met[32:64], chosen >> 1)
    )
    answers = jnp.concatenate([met[64:96], met[96:]], axis=1)
    answers = jnp.concatenate(split3(answers), axis=0)
    targets = jnp.concatenate(trace_q, axis=1).astype(jnp.int16)
    targets = jnp.broadcast_to(targets, (256, 256))
    for t in range(LOCAL // 256):
        row = lax.broadcasted_iota(jnp.int16, (256, 256), 0) + jnp.int16(t * 256)
        hot = jnp.where(row == targets, jnp.ones((256, 256), BF16), jnp.zeros((256, 256), BF16))
        put = lax.dot_general(answers, hot, NT, preferred_element_type=F32)
        here = slice(t * 256, t * 256 + 256)
        image[:, here] = image[:, here] + put[:32] + put[32:64] + put[64:]
    for p in range(2):
        for a, x in enumerate(split2(image[p * 16 : p * 16 + 16, :LOCAL])):
            zp[p, a * 48 + 32 : a * 48 + 48, :LOCAL] = x

    def inner(columns):
        made = jnp.zeros((96, 32), F32)
        for p in range(2):
            images = jnp.concatenate([zp[p, 32:48, columns], zp[p, 80:96, columns]], axis=0)
            made = made + lax.dot_general(
                zp[p, :, columns], images, NT, preferred_element_type=F32
            )
        return made[:48] + made[48:]

    pack[...] = jnp.zeros((48, 128), F32)
    pack[:, :32] = inner(slice(0, LOCAL))
    wait_bytes(arrived.at[pl.ds(0, COLS - 1)], part_recv)
    bem_image = taken
    for k in range(COLS):
        bem_image = bem_image + arrived[k]
    for p in range(2):
        for a, x in enumerate(split2(bem_image[p * 16 : p * 16 + 16, :])):
            zp[p, a * 48 + 32 : a * 48 + 48, LOCAL:] = x
    pack[:, :32] = pack[:, :32] + inner(slice(LOCAL, WIDE))
    sum_out[:8, :] = gathered(6, 16)
    reduce_cols()
    leave = pltpu.make_async_copy(zp, z_hbm, out_sem)
    leave.start()

    for d, (exists, _, _, _) in enumerate(neighbours):

        @pl.when(exists)
        def _(d=d):
            wait_bytes(halo_out.at[d], halo_send.at[d])

    wait_bytes(phi.at[:, pl.ds(0, (ROWS - 1) * PIECE)], phi_send)
    wait_bytes(arrived.at[pl.ds(0, COLS - 1)], part_send)
    wait_bytes(swap_mid.at[pl.ds(0, ROWS - 1)], mid_send)
    wait_bytes(swap_in.at[:, pl.ds(0, COLS - 1), :], swap_send)
    reduce_rows()
    wait_bytes(col_in.at[pl.ds(0, COLS - 1)], col_send)
    leave.wait()
    sums[...] = reduced()
    wait_bytes(row_in.at[pl.ds(0, ROWS - 1)], row_send)


def finish_kernel(
    z_hbm, sums, next_fem, next_bem, hess, rfac,
    zp, pack_q, pack, wide, fem_out, bem_out, in_sem, out_sem,
):
    copies = [pltpu.make_async_copy(z_hbm.at[p], zp.at[p], in_sem.at[p]) for p in range(2)]
    for copy in copies:
        copy.start()

    total = sums[8:, :]
    for g in range(4):
        pack_q[8 * g : 8 * g + 8, :] = total if g == 0 else pltpu.roll(total, 128 - 32 * g, 1)
    gram_q = pack_q[:, :32]
    total = sums[:8, :]
    for g in range(6):
        pack[8 * g : 8 * g + 8, :] = total if g == 0 else pltpu.roll(total, 128 - 16 * g, 1)
    one = pack[:32, :16]
    norm = pack[32:48, :16]

    both = 2.0 * one - small_dot(gram_q, one, ((1,), (0,)))
    hess[...] = both
    left = small_dot(gram_q, both, ((1,), (0,))) - one
    gram = norm + small_dot(both, left, ((0,), (0,))) - small_dot(one, both, ((0,), (0,)))
    row_id = lax.broadcasted_iota(jnp.int32, (16, 128), 0)
    col_id = lax.broadcasted_iota(jnp.int32, (16, 128), 1)
    wide[...] = (col_id == row_id + 16).astype(F32)
    wide[:, :16] = (gram + gram.T) * 0.5
    work = wide[...]
    rows = jnp.zeros((16, 128), F32)
    for j in range(0, 16, 2):
        line_a = jnp.broadcast_to(work[j : j + 1, :], (16, 128))
        line_b = jnp.broadcast_to(work[j + 1 : j + 2, :], (16, 128))
        col_a = jnp.broadcast_to(work[:, j : j + 1], (16, 128))
        col_b = jnp.broadcast_to(work[:, j + 1 : j + 2], (16, 128))
        aa = jnp.broadcast_to(col_a[j : j + 1, :], (16, 128))
        ab = jnp.broadcast_to(col_b[j : j + 1, :], (16, 128))
        bb = jnp.broadcast_to(col_b[j + 1 : j + 2, :], (16, 128))
        second = line_b - line_a * (ab / aa)
        rows = jnp.where(row_id == j, line_a, jnp.where(row_id == j + 1, second, rows))
        if j < 14:
            scale = 1.0 / (bb - ab * (ab / aa))
            step = (col_b - col_a * (ab / aa)) * scale
            work = work - col_a * (line_a / aa) - step * second
    pivot = jnp.sum(jnp.where(row_id == col_id, rows, 0.0), axis=1, keepdims=True)
    root = lax.rsqrt(pivot)
    root = root * (1.5 - 0.5 * pivot * root * root)
    rows = rows * root
    wide[...] = jnp.where(row_id <= col_id, rows, 0.0)
    rfac[...] = wide[:, :16]
    wide[...] = pltpu.roll(rows, 112, 1)
    lower_inv = wide[:, :16]

    weights = -small_dot(lower_inv, both, ((1,), (1,)))
    w_pair = jnp.concatenate(split2(weights), axis=0)
    l_pair = jnp.concatenate(split2(lower_inv), axis=0)
    leaving = []
    for p in range(2):
        copies[p].wait()
        first = jnp.dot(w_pair, zp[p, :32, :], preferred_element_type=F32)
        first = first + jnp.dot(l_pair, zp[p, 32:48, :], preferred_element_type=F32)
        second = jnp.dot(w_pair[:16], zp[p, 48:80, :], preferred_element_type=F32)
        second = second + jnp.dot(l_pair[:16], zp[p, 80:, :], preferred_element_type=F32)
        made = first[:16] + first[16:] + second
        fem_out[p] = made[:, :LOCAL]
        bem_out[p] = made[:, LOCAL:]
        leaving.append(pltpu.make_async_copy(fem_out.at[p], next_fem.at[:, p, :], out_sem.at[p]))
        leaving.append(
            pltpu.make_async_copy(bem_out.at[p], next_bem.at[:, p, :], out_sem.at[2 + p])
        )
        leaving[-2].start()
        leaving[-1].start()
    for copy in leaving:
        copy.wait()


def body(fem_basis, bem_basis, diag, vals, cols, halo, mat, trace, slot):
    vmem = pl.BlockSpec(memory_space=pltpu.VMEM)
    hbm = pl.BlockSpec(memory_space=pl.ANY)
    dma = pltpu.SemaphoreType.DMA
    halves, sums = pl.pallas_call(
        step_kernel,
        out_shape=(
            jax.ShapeDtypeStruct((2, 96, WIDE), BF16),
            jax.ShapeDtypeStruct((16, 128), F32),
        ),
        in_specs=[hbm] * 9,
        out_specs=(hbm, vmem),
        scratch_shapes=[
            pltpu.VMEM((2, VEC, LOCAL), F32),
            pltpu.VMEM((2, VEC, PIECE), F32),
            pltpu.VMEM((1, LOCAL), F32),
            pltpu.VMEM((16, LOCAL), F32),
            pltpu.VMEM((16, LOCAL), jnp.int32),
            pltpu.VMEM((4, 128), jnp.int32),
            pltpu.VMEM((1, 256), jnp.int32),
            pltpu.VMEM((1, PIECE), jnp.int32),
            dma((20,)),
            dma,
            pltpu.VMEM((640, 256), BF16),
            pltpu.VMEM((16, 2560), jnp.int32),
            pltpu.VMEM((VEC, 1), F32),
            pltpu.VMEM((4, VEC, 128), F32),
            pltpu.VMEM((4, VEC, 128), F32),
            pltpu.VMEM((VEC, ROWS * PIECE), BF16),
            pltpu.VMEM((COLS, VEC, PIECE), F32),
            pltpu.VMEM((COLS, VEC, PIECE), F32),
            pltpu.VMEM((DEVICES, 128), F32),
            pltpu.VMEM((ROWS, COLS, 128), F32),
            pltpu.VMEM((ROWS, COLS, 128), F32),
            pltpu.VMEM((2, 2048, 1024), BF16),
            pltpu.VMEM((VEC, LOCAL), F32),
            pltpu.VMEM((2, 96, WIDE), BF16),
            pltpu.VMEM((48, 128), F32),
            pltpu.VMEM((16, 128), F32),
            pltpu.VMEM((COLS, 16, 128), F32),
            pltpu.VMEM((ROWS, 16, 128), F32),
            dma((8,)),
            dma((4,)),
            dma((4,)),
            dma, dma, dma, dma, dma, dma, dma, dma,
            dma, dma, dma, dma,
        ],
        compiler_params=pltpu.CompilerParams(
            has_side_effects=True, collective_id=0, vmem_limit_bytes=60 << 20
        ),
    )(fem_basis, bem_basis, diag.reshape(1, LOCAL), vals, cols, halo, mat, trace.reshape(1, 256), slot.reshape(1, PIECE))
    next_fem, next_bem, hess, rfac = pl.pallas_call(
        finish_kernel,
        out_shape=(
            jax.ShapeDtypeStruct((16, 2, LOCAL), F32),
            jax.ShapeDtypeStruct((16, 2, PIECE), F32),
            jax.ShapeDtypeStruct((VEC, 16), F32),
            jax.ShapeDtypeStruct((16, 16), F32),
        ),
        in_specs=[hbm, vmem],
        out_specs=(hbm, hbm, vmem, vmem),
        scratch_shapes=[
            pltpu.VMEM((2, 96, WIDE), BF16),
            pltpu.VMEM((VEC, 128), F32),
            pltpu.VMEM((48, 128), F32),
            pltpu.VMEM((16, 128), F32),
            pltpu.VMEM((2, 16, LOCAL), F32),
            pltpu.VMEM((2, 16, PIECE), F32),
            dma((2,)),
            dma((4,)),
        ],
        compiler_params=pltpu.CompilerParams(vmem_limit_bytes=60 << 20),
    )(halves, sums)
    return next_fem, next_bem, hess.reshape(2, 16, 16), rfac


def solution(mesh):
    both = ("row", "col")
    return jax.shard_map(
        body,
        mesh=mesh,
        in_specs=(
            P(None, None, None, both), P(None, None, None, both), P(both), P(None, both),
            P(None, both), P(None, both), P(None, "row", "col"), P(both), P(both),
        ),
        out_specs=(P(None, None, both), P(None, None, both), P(), P()),
        check_vma=False,
    )
```
